32 devices in a mesh: section: 1, expert: 32 (over z, y, x, core).
Axes of the slice: x: 2, y: 2, z: 4, core: 2. Of those that a mesh axis runs over, the one named last changes fastest.
Arguments:
- hidden: bfloat16 [1, 256, 7168], P('section', 'expert'), may hold values from -6 to 6
- norm_gain: float32 [1, 7168], P('section'), may hold values from 0.25 to 1.75
- w_up: bfloat16 [1, 7168, 4096], P('section', None, 'expert'), may hold values from -0.0625 to 0.0625
- w_down: bfloat16 [1, 4096, 7168], P('section', 'expert'), may hold values from -0.1875 to 0.1875
- expert_ids: int32 [1, 2, 256, 2], P('section', None, 'expert'), may hold values from 0 to 3, all different within a row; in each aligned block of 8 rows (0 to 7, 8 to 15, ..., all dimensions but the last counted through in order) at most 6 rows name the same one
- route_gates: float32 [1, 2, 256, 2], P('section', None, 'expert'), may hold values from 0.25 to 1.5
Outputs:
- advanced: bfloat16 [1, 256, 7168], P('section', 'expert')
The draws below stay inside these ranges and needn't reach their ends.
Inputs may be any that keep to these rules, and one draw needn't show every extreme that they name: `expert_ids`: the 2 ids of a row differ. In each aligned block of 8 rows (the rows of one device in one pass) no expert is named by more than 6 rows; some expert is named by exactly 6 rows.
All inputs are finite; a program needn't handle non-finite values.
Results may differ from the reference program's by a relative error of at most 0.0085.
Values may be sent and summed in bfloat16 or wider, within the bound.
A program may use at most 64 MiB of HBM per device.

```python
import math
import jax
import jax.numpy as jnp
import numpy as np
from jax import lax

D = 7168
HID = 1024
HID_DEV = 128
TOP = 2
ITERS = 2
ROWS_DEV = 8
GROUP = 8
EXPERTS_SECTION = 4
CAP = 6
MBROWS = 256
SECTIONS = 1
N_EXPERT = 32


def block_levels(rng, extent, shards, least, largest):
    loudness = 1.0
    for dim, blocks in shards:
        steps = jax.random.uniform(jax.random.fold_in(jax.random.fold_in(rng, 6), dim), (blocks,), jnp.float32, least / len(shards), largest / len(shards))
        loudness = loudness * jnp.repeat(jnp.exp(steps), extent[dim] // blocks).reshape((-1,) + (1,) * (len(extent) - 1 - dim))
    return loudness


def routed_block(own_key, own, number, rows, count, top, reach, lean):
    ranking = jax.random.permutation(own_key, count)
    crowded, usual = load_shares(count, rows * top, reach, lean, True), load_shares(count, rows * top, reach, lean, False)
    places = jnp.arange(count)

    def named(lengths, rotation):
        used = int((lengths > 0).sum())
        fixed = max(1, used // 4)
        passed = fixed + (places - fixed + rotation * (used - fixed)) % max(1, count - fixed)
        return jnp.zeros((count,), jnp.int32).at[ranking[jnp.where(places < fixed, places, passed)]].set(jnp.asarray(lengths, jnp.int32))

    lengths = jnp.where(number % 4 == 0, named(crowded, number // 4), named(usual, number - number // 4 - 1))
    mixed = jax.random.permutation(jax.random.fold_in(own, 3), count)
    source_of, receiver = mixed[0:count // 2 * 2:2], mixed[1:count // 2 * 2:2]
    room = jnp.minimum(lengths[source_of] - 1, reach - lengths[receiver]) // 2
    room = jnp.where((source_of == ranking[0]) | (receiver == ranking[0]) | (lengths[receiver] == 0), 0, jnp.maximum(room, 0))
    passed = jax.random.randint(jax.random.fold_in(own, 4), (count // 2,), 0, 1 << 20) % (room + 1)
    lengths = lengths.at[source_of].add(-passed).at[receiver].add(passed)
    items = jnp.searchsorted(jnp.cumsum(lengths), jnp.arange(rows * top), side="right").astype(jnp.int32)
    grid = items.reshape(top, rows).T
    grid = grid[jax.random.permutation(jax.random.fold_in(own, 1), rows)]
    rotation = jax.random.randint(jax.random.fold_in(own, 2), (rows, 1), 0, top)
    return jnp.take_along_axis(grid, (jnp.arange(top)[None, :] + rotation) % top, axis=1)


def load_shares(amount, total, reach, skew, full):
    portions = [(1 << 20) // math.isqrt(rank ** skew) + 1 for rank in range(1, amount + 1)]
    largest = reach if full else min(reach, max(-(-total // amount), total * portions[0] // sum(portions)))
    least = 1 if total - largest >= amount - 1 else 0
    counts, surplus = [largest] + [least] * (amount - 1), total - largest - least * (amount - 1)
    while surplus > 0:
        candidates = [i for i in range(1, amount) if counts[i] < largest] or [i for i in range(1, amount) if counts[i] < reach]
        mass, budget = sum([portions[i] for i in candidates]), surplus
        for i in candidates:
            addition = min(reach - counts[i], max(1, budget * portions[i] // mass), surplus)
            counts[i] = counts[i] + addition
            surplus = surplus - addition
    return np.array(counts)


def bell_draw(key, extent, width, reach, cuts=(), held_as=jnp.bfloat16):
    result = jax.random.normal(key, extent, jnp.float32) * width
    if len(cuts) > 0:
        result = block_levels(key, extent, cuts, -0.22, 0.18) * result
    return jnp.clip(result, min=-reach, max=reach).astype(held_as)


def setup_inputs(seed: int = 0) -> dict:
    seeds = jax.random.split(jax.random.key(seed), 7)
    hidden = bell_draw(seeds[0], (SECTIONS, MBROWS, D), 1.0, 6.0, ((1, 32),))
    norm_gain = jnp.clip(1.0 + 0.15 * jax.random.normal(seeds[1], (SECTIONS, D), jnp.float32), 0.25, 1.75)
    w_up = bell_draw(seeds[2], (SECTIONS, D, EXPERTS_SECTION * HID), D ** -0.5, 0.0625, ((2, 32),))
    w_down = bell_draw(seeds[3], (SECTIONS, EXPERTS_SECTION * HID, D), HID ** -0.5, 0.1875, ((1, 32),))
    expert_ids_keys = jax.random.split(jax.random.fold_in(seeds[4], 1), SECTIONS * ITERS * MBROWS // ROWS_DEV)
    expert_ids_turns = jax.random.permutation(jax.random.fold_in(seeds[4], 3), SECTIONS * ITERS * MBROWS // ROWS_DEV)
    expert_ids = jax.vmap(lambda own, number: routed_block(jax.random.fold_in(seeds[4], 2), own, number, ROWS_DEV, EXPERTS_SECTION, TOP, CAP, 2))(expert_ids_keys, expert_ids_turns).reshape((SECTIONS, ITERS, MBROWS, TOP))
    route_gates = jnp.clip(0.25 + 1.25 * jax.random.uniform(seeds[5], (SECTIONS, ITERS, MBROWS, TOP), jnp.float32) ** block_levels(seeds[5], (SECTIONS, ITERS, MBROWS, TOP), ((2, 32),), -0.2, 0.2), 0.25, 1.5)
    return {"hidden": hidden, "norm_gain": norm_gain, "w_up": w_up, "w_down": w_down, "expert_ids": expert_ids, "route_gates": route_gates}


def layer(operands):
    current, gain_row, up_weight, down_weight, route_ids, gate_values = operands
    values = current.astype(jnp.float32)
    inverse_rms = lax.rsqrt(lax.optimization_barrier(jnp.mean(values * values, axis=-1, keepdims=True)) + 1e-06)
    normed = (values * inverse_rms * gain_row.astype(jnp.float32)).astype(jnp.bfloat16)
    row_count = current.shape[0]
    top_count = route_ids.shape[1]
    slot_count = N_EXPERT * CAP
    flat_ids = route_ids.reshape(-1).astype(jnp.int32)
    onehot = (flat_ids[:, None] == jnp.arange(EXPERTS_SECTION, dtype=jnp.int32)[None, :]).astype(jnp.int32)
    earlier = jnp.cumsum(onehot, axis=0) - onehot
    slot_index = lax.optimization_barrier(jnp.sum(earlier * onehot, axis=1)).astype(jnp.int32)
    target = (flat_ids * slot_count + slot_index).astype(jnp.int32)
    source_rows = (jnp.arange(row_count * top_count, dtype=jnp.int32) // top_count).astype(jnp.int32)
    holder = jnp.zeros((EXPERTS_SECTION * slot_count,), jnp.int32).at[target].set(source_rows)
    filled = jnp.zeros((EXPERTS_SECTION * slot_count,), jnp.float32).at[target].set(1.0)
    gathered = normed[holder] * filled[:, None].astype(jnp.bfloat16)
    batches = gathered.reshape(EXPERTS_SECTION, slot_count, D)

    def one_expert(inputs):
        rows_in, expert_index = inputs
        up_part = lax.dynamic_slice_in_dim(up_weight, (expert_index * HID).astype(jnp.int32), HID, 1)
        down_part = lax.dynamic_slice_in_dim(down_weight, (expert_index * HID).astype(jnp.int32), HID, 0)
        upward = jnp.dot(rows_in, up_part, preferred_element_type=jnp.float32)
        active = jax.nn.silu(upward).astype(jnp.bfloat16)
        pieces = jnp.einsum('sgh,ghd->sgd', active.reshape(slot_count, GROUP, HID_DEV).astype(jnp.float32), down_part.reshape(GROUP, HID_DEV, D).astype(jnp.float32), precision=lax.Precision.HIGHEST)
        rounded = lax.optimization_barrier(pieces.astype(jnp.bfloat16))
        return lax.optimization_barrier(jnp.sum(rounded.astype(jnp.float32), axis=1))
    outputs = lax.map(one_expert, (batches, jnp.arange(EXPERTS_SECTION, dtype=jnp.int32)))
    chosen = outputs.reshape(-1, D)[target]
    weighted = chosen * gate_values.reshape(-1)[:, None].astype(jnp.float32)
    mixture = lax.optimization_barrier(jnp.sum(weighted.reshape(row_count, top_count, D), axis=1))
    return (values + mixture).astype(jnp.bfloat16)

def reference(hidden, norm_gain, w_up, w_down, expert_ids, route_gates):
    current = hidden
    for pass_index in range(ITERS):
        advanced = lax.map(layer, (current, norm_gain, w_up, w_down, expert_ids[:, pass_index], route_gates[:, pass_index]))
        current = jnp.roll(advanced, 1, axis=0)
    return current
```

```python
import functools

import jax
import jax.numpy as jnp
from jax import lax
from jax.experimental import pallas as pl
from jax.experimental.pallas import tpu as pltpu
from jax.sharding import PartitionSpec as P

HID = 1024
HID_DEV = 128
CHUNKS = 4
CHIPS = HID // HID_DEV // 2


def kernel(
    planes, sections, passes,
    hidden, gain, ids, gates, up_hbm, down_hbm, out,
    up, down, rows, meta, part, first, second_out, second, plane_sum, plane_in, cur, shift_out, shift_in,
    w_local, w_send, w_recv, meta_send, meta_recv, zag_send, zag_recv, pag_send, pag_recv,
    one_send, one_recv, two_send, two_recv, zrs_send, zrs_recv, sh_send, sh_recv,
):
    me = lax.axis_index("expert")
    core = lax.rem(me, 2)
    chip = lax.rem(me // 2, CHIPS)
    plane = me // (2 * CHIPS)
    half = cur.shape[2]
    wide = half // CHUNKS
    mate = {1: chip + 1 - 2 * lax.rem(chip, 2), 2: lax.rem(chip + 2, 4), 3: 3 - chip}

    def at(plane_index, chip_index, core_index):
        return {"expert": (plane_index * CHIPS + chip_index) * 2 + core_index}

    def plane_at(by):
        return lax.rem(plane + by + planes, planes)

    partner = at(plane, chip, 1 - core)
    peers = [at(plane_at(d), chip, core) for d in range(1, planes)]
    mates = {k: at(plane, mate[k], core) for k in (1, 2)}
    targets = [partner, mates[1], mates[2]] + peers
    if sections > 1:
        sec = lax.axis_index("section")
        after = {"section": lax.rem(sec + 1, sections)}
        before = {"section": lax.rem(sec + sections - 1, sections)}
        targets = targets + [after, before]
    barrier = pltpu.get_barrier_semaphore()
    for target in targets:
        pl.semaphore_signal(barrier, inc=1, device_id=target, device_id_type=pl.DeviceIdType.MESH)
    pl.semaphore_wait(barrier, len(targets))

    pending = []

    def remote(src, dst, send, recv, target):
        return pltpu.make_async_remote_copy(
            src_ref=src, dst_ref=dst, send_sem=send, recv_sem=recv,
            device_id=target, device_id_type=pl.DeviceIdType.MESH,
        )

    def send(*args):
        copy = remote(*args)
        copy.start()
        pending.append(copy)

    lanes = lax.broadcasted_iota(jnp.int32, (ids.shape[1], 128), 1)
    table = jnp.zeros((ids.shape[1], 128), jnp.float32)
    for p in range(passes):
        for k in range(ids.shape[2]):
            hit = lanes == ids[p, :, k : k + 1] + p * planes
            table = table + jnp.where(hit, gates[p, :, k : k + 1], 0.0)
    meta[chip, plane] = table
    for d in range(1, planes):
        send(meta.at[chip, plane], meta.at[chip, plane], meta_send.at[d - 1], meta_recv.at[d - 1], peers[d - 1])

    for h in range(2):
        cur[h] = hidden[:, h * half : (h + 1) * half].astype(jnp.float32)

    def gather_z(p):
        a, b = cur[0], cur[1]
        total = jnp.sum(a * a, axis=-1, keepdims=True) + jnp.sum(b * b, axis=-1, keepdims=True)
        scale = lax.rsqrt(total / (2 * half) + 1e-06)
        for c in range(CHUNKS):
            lo, hi = c * wide, (c + 1) * wide
            top = cur[0, :, lo:hi] * scale * gain[:, lo:hi]
            bottom = cur[1, :, lo:hi] * scale * gain[:, half + lo : half + hi]
            rows[p, c, chip, plane] = jnp.concatenate([top, bottom], axis=0).astype(jnp.bfloat16)
            block = rows.at[p, c, chip, plane]
            for d in range(1, planes):
                send(block, block, zag_send.at[p, c, d - 1], zag_recv.at[p, c, d - 1], peers[d - 1])

    def order(c):
        return (1, 2) if c % 2 == 0 else (2, 1)

    gather_z(0)
    locals_ = [
        pltpu.make_async_copy(up_hbm, up.at[:, pl.ds(0, HID_DEV)], w_local.at[0]),
        pltpu.make_async_copy(down_hbm, down.at[pl.ds(0, HID_DEV)], w_local.at[1]),
    ]
    for copy in locals_:
        copy.start()
    up_copy = remote(up_hbm, up.at[:, pl.ds(HID_DEV, HID_DEV)], w_send.at[0], w_recv.at[0], partner)
    down_copy = remote(down_hbm, down.at[pl.ds(HID_DEV, HID_DEV)], w_send.at[1], w_recv.at[1], partner)
    up_copy.start()
    down_copy.start()

    for d in range(1, planes):
        src = meta.at[chip, plane_at(-d)]
        remote(src, src, meta_send.at[d - 1], meta_recv.at[d - 1], peers[d - 1]).wait_recv()
    slot = planes - 1
    for i, k in enumerate((1, 2)):
        send(meta.at[chip], meta.at[chip], meta_send.at[slot + i], meta_recv.at[slot + i], mates[k])

    def meta_forward():
        src = meta.at[mate[1]]
        remote(src, src, meta_send.at[slot], meta_recv.at[slot], mates[1]).wait_recv()
        send(src, src, meta_send.at[slot + 2], meta_recv.at[slot + 2], mates[2])

    def meta_finish():
        for i, k in ((1, 2), (2, 3)):
            src = meta.at[mate[k]]
            remote(src, src, meta_send.at[slot + i], meta_recv.at[slot + i], mates[2]).wait_recv()

    for p in range(passes):
        if p > 0:
            gather_z(p)
        top_sum = bottom_sum = None
        for step in range(CHUNKS + 2):
            if step < CHUNKS:
                c = step
                for d in range(1, planes):
                    src = rows.at[p, c, chip, plane_at(-d)]
                    remote(src, src, zag_send.at[p, c, d - 1], zag_recv.at[p, c, d - 1], peers[d - 1]).wait_recv()
                for i, k in enumerate(order(c)):
                    src = rows.at[p, c, chip]
                    send(src, src, pag_send.at[p, c, i], pag_recv.at[p, c, i], mates[k])
            if 1 <= step <= CHUNKS:
                c = step - 1
                near, far = order(c)
                src = rows.at[p, c, mate[near]]
                remote(src, src, pag_send.at[p, c, 0], pag_recv.at[p, c, 0], mates[near]).wait_recv()
                send(src, src, pag_send.at[p, c, 2], pag_recv.at[p, c, 2], mates[far])
                if p == 0 and step == 1:
                    meta_forward()
            if step >= 2:
                c = step - 2
                near, far = order(c)
                for i, k in ((1, far), (2, 3)):
                    src = rows.at[p, c, mate[k]]
                    remote(src, src, pag_send.at[p, c, i], pag_recv.at[p, c, i], mates[far]).wait_recv()
                if p == 0 and c == 0:
                    locals_[0].wait()
                    up_copy.wait_recv()
                block = rows[p, c].reshape(CHIPS * planes * 16, wide)
                top = jnp.dot(block, up[c * wide : (c + 1) * wide, :], preferred_element_type=jnp.float32)
                bottom = jnp.dot(
                    block, up[half + c * wide : half + (c + 1) * wide, :], preferred_element_type=jnp.float32
                )
                top_sum = top if c == 0 else top_sum + top
                bottom_sum = bottom if c == 0 else bottom_sum + bottom
        if p == 0:
            meta_finish()
            locals_[1].wait()
            down_copy.wait_recv()
        upward = (
            top_sum.reshape(CHIPS * planes, 2, 8, 2 * HID_DEV)[:, 0]
            + bottom_sum.reshape(CHIPS * planes, 2, 8, 2 * HID_DEV)[:, 1]
        ).reshape(CHIPS * planes * 8, 2 * HID_DEV)
        tables = meta[...].reshape(CHIPS * planes * 8, 128)
        mine = lax.broadcasted_iota(jnp.int32, tables.shape, 1) == plane + p * planes
        gate = jnp.sum(jnp.where(mine, tables, 0.0), axis=-1, keepdims=True)
        active = (upward / (1.0 + jnp.exp(-upward)) * gate).astype(jnp.bfloat16)
        for c in range(CHUNKS):
            lo, hi = c * wide, (c + 1) * wide
            top = jnp.dot(active, down[:, lo:hi], preferred_element_type=jnp.float32)
            bottom = jnp.dot(active, down[:, half + lo : half + hi], preferred_element_type=jnp.float32)
            both = jnp.concatenate(
                [top.reshape(CHIPS * planes, 8, wide), bottom.reshape(CHIPS * planes, 8, wide)], axis=1
            )
            part[p, c] = both.astype(jnp.bfloat16).reshape(CHIPS, planes, 16, wide)
            near, far = order(c)
            for i, k in ((1, 3), (0, near)):
                send(
                    part.at[p, c, mate[k]], first.at[p, c, i], one_send.at[p, c, i], one_recv.at[p, c, i], mates[near]
                )
        for step in range(CHUNKS + 1):
            if step < CHUNKS:
                c = step
                near, far = order(c)
                src = first.at[p, c, 1]
                remote(src, src, one_send.at[p, c, 1], one_recv.at[p, c, 1], mates[near]).wait_recv()
                total = part[p, c, mate[far]].astype(jnp.float32) + first[p, c, 1].astype(jnp.float32)
                second_out[p, c] = total.astype(jnp.bfloat16)
                send(second_out.at[p, c], second.at[p, c], two_send.at[p, c], two_recv.at[p, c], mates[far])
            if step >= 1:
                c = step - 1
                near, far = order(c)
                src = first.at[p, c, 0]
                remote(src, src, one_send.at[p, c, 0], one_recv.at[p, c, 0], mates[near]).wait_recv()
                src = second.at[p, c]
                remote(src, src, two_send.at[p, c], two_recv.at[p, c], mates[far]).wait_recv()
                total = part[p, c, chip].astype(jnp.float32) + first[p, c, 0].astype(jnp.float32)
                total = total + second[p, c].astype(jnp.float32)
                plane_sum[p, c] = total.astype(jnp.bfloat16)
                for d in range(1, planes):
                    send(
                        plane_sum.at[p, c, plane_at(d)], plane_in.at[p, c, d - 1],
                        zrs_send.at[p, c, d - 1], zrs_recv.at[p, c, d - 1], peers[d - 1],
                    )
        for c in range(CHUNKS):
            lo, hi = c * wide, (c + 1) * wide
            total = plane_sum[p, c, plane].astype(jnp.float32)
            for d in range(1, planes):
                src = plane_in.at[p, c, d - 1]
                remote(src, src, zrs_send.at[p, c, d - 1], zrs_recv.at[p, c, d - 1], peers[d - 1]).wait_recv()
                total = total + plane_in[p, c, d - 1].astype(jnp.float32)
            for h in range(2):
                value = (cur[h, :, lo:hi] + total[h * 8 : h * 8 + 8]).astype(jnp.bfloat16).astype(jnp.float32)
                cur[h, :, lo:hi] = value
        if sections > 1:
            shift_out[p] = jnp.concatenate([cur[0], cur[1]], axis=0).astype(jnp.bfloat16)
            send(shift_out.at[p], shift_in.at[p], sh_send.at[p], sh_recv.at[p], after)
            remote(shift_out.at[p], shift_in.at[p], sh_send.at[p], sh_recv.at[p], after).wait_recv()
            for h in range(2):
                cur[h] = shift_in[p].astype(jnp.float32)[h * 8 : h * 8 + 8]
    for h in range(2):
        out[:, h * half : (h + 1) * half] = cur[h].astype(jnp.bfloat16)
    up_copy.wait_send()
    down_copy.wait_send()
    for copy in pending:
        copy.wait_send()


def body(hidden, norm_gain, w_up, w_down, expert_ids, route_gates):
    width = hidden.shape[-1]
    half = width // 2
    wide = half // CHUNKS
    planes = lax.axis_size("expert") // (2 * CHIPS)
    sections = lax.axis_size("section")
    passes = expert_ids.shape[1]
    bf = jnp.bfloat16
    dma = pltpu.SemaphoreType.DMA
    away = planes - 1
    shift = passes if sections > 1 else 1
    vmem = pl.BlockSpec(memory_space=pltpu.VMEM)
    hbm = pl.BlockSpec(memory_space=pl.ANY)
    result = pl.pallas_call(
        functools.partial(kernel, planes, sections, passes),
        out_shape=jax.ShapeDtypeStruct((8, width), bf),
        in_specs=[vmem] * 4 + [hbm] * 2,
        out_specs=vmem,
        scratch_shapes=[
            pltpu.VMEM((width, 2 * HID_DEV), bf),
            pltpu.VMEM((2 * HID_DEV, width), bf),
            pltpu.VMEM((passes, CHUNKS, CHIPS, planes, 16, wide), bf),
            pltpu.VMEM((CHIPS, planes, 8, 128), jnp.float32),
            pltpu.VMEM((passes, CHUNKS, CHIPS, planes, 16, wide), bf),
            pltpu.VMEM((passes, CHUNKS, 2, planes, 16, wide), bf),
            pltpu.VMEM((passes, CHUNKS, planes, 16, wide), bf),
            pltpu.VMEM((passes, CHUNKS, planes, 16, wide), bf),
            pltpu.VMEM((passes, CHUNKS, planes, 16, wide), bf),
            pltpu.VMEM((passes, CHUNKS, away, 16, wide), bf),
            pltpu.VMEM((2, 8, half), jnp.float32),
            pltpu.VMEM((shift, 16, half), bf),
            pltpu.VMEM((shift, 16, half), bf),
            dma((2,)), dma((2,)), dma((2,)),
            dma((away + 3,)), dma((away + 3,)),
            dma((passes, CHUNKS, away)), dma((passes, CHUNKS, away)),
            dma((passes, CHUNKS, 3)), dma((passes, CHUNKS, 3)),
            dma((passes, CHUNKS, 2)), dma((passes, CHUNKS, 2)),
            dma((passes, CHUNKS)), dma((passes, CHUNKS)),
            dma((passes, CHUNKS, away)), dma((passes, CHUNKS, away)),
            dma((shift,)), dma((shift,)),
        ],
        compiler_params=pltpu.CompilerParams(
            collective_id=0, has_side_effects=True, vmem_limit_bytes=56 * 1024 * 1024
        ),
    )(hidden[0], norm_gain, expert_ids[0], route_gates[0], w_up[0], w_down[0])
    return result[None]


def solution(mesh):
    placed = (
        P("section", "expert", None),
        P("section", None),
        P("section", None, "expert"),
        P("section", "expert", None),
        P("section", None, "expert", None),
        P("section", None, "expert", None),
    )
    return jax.shard_map(
        body, mesh=mesh, in_specs=placed, out_specs=P("section", "expert", None), check_vma=False
    )
```

```python
import functools

import jax
import jax.numpy as jnp
from jax import lax
from jax.experimental import pallas as pl
from jax.experimental.pallas import tpu as pltpu
from jax.sharding import PartitionSpec as P

HID = 1024
HID_DEV = 128
CHUNKS = 4
CHIPS = HID // HID_DEV // 2


def kernel(
    planes, sections, passes, cap,
    hidden, gain, ids, gates, up_hbm, down_hbm, out,
    up, down, column, rows, meta, slot_gates, part, first, second_out, second, plane_sum, plane_in, cur, shift_out, shift_in,
    w_local, w_send, w_recv, meta_send, meta_recv, zag_send, zag_recv, pag_send, pag_recv,
    one_send, one_recv, two_send, two_recv, zrs_send, zrs_recv, sh_send, sh_recv,
):
    me = lax.axis_index("expert")
    core = lax.rem(me, 2)
    chip = lax.rem(me // 2, CHIPS)
    plane = me // (2 * CHIPS)
    half = cur.shape[2]
    wide = half // CHUNKS
    mate = {1: chip + 1 - 2 * lax.rem(chip, 2), 2: lax.rem(chip + 2, 4), 3: 3 - chip}

    def at(plane_index, chip_index, core_index):
        return {"expert": (plane_index * CHIPS + chip_index) * 2 + core_index}

    def plane_at(by):
        return lax.rem(plane + by + planes, planes)

    partner = at(plane, chip, 1 - core)
    peers = [at(plane_at(d), chip, core) for d in range(1, planes)]
    mates = {k: at(plane, mate[k], core) for k in (1, 2)}
    targets = [partner, mates[1], mates[2]] + peers
    if sections > 1:
        sec = lax.axis_index("section")
        after = {"section": lax.rem(sec + 1, sections)}
        before = {"section": lax.rem(sec + sections - 1, sections)}
        targets = targets + [after, before]
    barrier = pltpu.get_barrier_semaphore()
    for target in targets:
        pl.semaphore_signal(barrier, inc=1, device_id=target, device_id_type=pl.DeviceIdType.MESH)
    pl.semaphore_wait(barrier, len(targets))

    pending = []

    def remote(src, dst, send, recv, target):
        return pltpu.make_async_remote_copy(
            src_ref=src, dst_ref=dst, send_sem=send, recv_sem=recv,
            device_id=target, device_id_type=pl.DeviceIdType.MESH,
        )

    def send(*args):
        copy = remote(*args)
        copy.start()
        pending.append(copy)

    lanes = lax.broadcasted_iota(jnp.int32, (8, 128), 1)
    diagonal = lax.broadcasted_iota(jnp.int32, (8, 8), 0) == lax.broadcasted_iota(jnp.int32, (8, 8), 1)
    table = jnp.zeros((8, 128), jnp.float32)
    for p in range(passes):
        for k in range(ids.shape[1]):
            named = jnp.sum(jnp.where(diagonal, ids[p, k : k + 1, :], 0).astype(jnp.float32), axis=-1, keepdims=True)
            weight = jnp.sum(jnp.where(diagonal, gates[p, k : k + 1, :], 0.0), axis=-1, keepdims=True)
            hit = lanes == named.astype(jnp.int32) + p * planes
            table = table + jnp.where(hit, weight, 0.0)
    meta[plane] = table
    for d in range(1, planes):
        send(meta.at[plane], meta.at[plane], meta_send.at[d - 1], meta_recv.at[d - 1], peers[d - 1])

    for h in range(2):
        cur[h] = hidden[:, h * half : (h + 1) * half].astype(jnp.float32)

    def gather_z(p):
        a, b = cur[0], cur[1]
        total = jnp.sum(a * a, axis=-1, keepdims=True) + jnp.sum(b * b, axis=-1, keepdims=True)
        scale = lax.rsqrt(total / (2 * half) + 1e-06)
        for c in range(CHUNKS):
            lo, hi = c * wide, (c + 1) * wide
            top = cur[0, :, lo:hi] * scale * gain[:, lo:hi]
            bottom = cur[1, :, lo:hi] * scale * gain[:, half + lo : half + hi]
            column[p, c, plane] = jnp.concatenate([top, bottom], axis=0).astype(jnp.bfloat16)
            block = column.at[p, c, plane]
            for d in range(1, planes):
                send(block, block, zag_send.at[p, c, d - 1], zag_recv.at[p, c, d - 1], peers[d - 1])

    def order(c):
        return (1, 2) if c % 2 == 0 else (2, 1)

    gather_z(0)
    locals_ = [
        pltpu.make_async_copy(up_hbm, up.at[:, pl.ds(0, HID_DEV)], w_local.at[0]),
        pltpu.make_async_copy(down_hbm, down.at[pl.ds(0, HID_DEV)], w_local.at[1]),
    ]
    for copy in locals_:
        copy.start()
    up_copy = remote(up_hbm, up.at[:, pl.ds(HID_DEV, HID_DEV)], w_send.at[0], w_recv.at[0], partner)
    down_copy = remote(down_hbm, down.at[pl.ds(HID_DEV, HID_DEV)], w_send.at[1], w_recv.at[1], partner)
    up_copy.start()
    down_copy.start()

    for d in range(1, planes):
        src = meta.at[plane_at(-d)]
        remote(src, src, meta_send.at[d - 1], meta_recv.at[d - 1], peers[d - 1]).wait_recv()
    slots = planes * cap
    count = planes * 16
    unpackers, packers = [], []
    gate_lanes = jnp.zeros((slots, 128), jnp.float32)
    for p in range(passes):
        pieces = []
        for g in range(planes):
            gate = jnp.sum(jnp.where(lanes == plane + p * planes, meta[g], 0.0), axis=-1, keepdims=True)
            routed = jnp.where(gate != 0.0, 1.0, 0.0)
            earlier = jnp.sum(
                jnp.where(
                    lax.broadcasted_iota(jnp.int32, (8, 8), 0) < lax.broadcasted_iota(jnp.int32, (8, 8), 1), routed, 0.0
                ),
                axis=0, keepdims=True,
            )
            place = jnp.sum(jnp.where(diagonal, earlier, 0.0), axis=-1, keepdims=True).astype(jnp.int32)
            for h in range(2):
                pieces.append(jnp.where(lanes == place + (h * slots + g * cap), gate, 0.0))
        if count < 128:
            pieces.append(jnp.zeros((128 - count, 128), jnp.float32))
        spread = jnp.concatenate(pieces, axis=0)
        turned = spread.T
        unpackers.append(jnp.where(spread[:count, : 2 * slots] != 0.0, 1.0, 0.0).astype(jnp.bfloat16))
        packers.append(jnp.where(turned[: 2 * slots, :count] != 0.0, 1.0, 0.0).astype(jnp.bfloat16))
        slot_gate = jnp.sum(turned[:slots], axis=-1, keepdims=True)
        gate_lanes = gate_lanes + jnp.where(lax.broadcasted_iota(jnp.int32, (slots, 128), 1) == p, slot_gate, 0.0)
    slot_gates[chip] = gate_lanes
    slot = planes - 1
    for i, k in enumerate((1, 2)):
        send(slot_gates.at[chip], slot_gates.at[chip], meta_send.at[slot + i], meta_recv.at[slot + i], mates[k])

    def meta_forward():
        src = slot_gates.at[mate[1]]
        remote(src, src, meta_send.at[slot], meta_recv.at[slot], mates[1]).wait_recv()
        send(src, src, meta_send.at[slot + 2], meta_recv.at[slot + 2], mates[2])

    def meta_finish():
        for i, k in ((1, 2), (2, 3)):
            src = slot_gates.at[mate[k]]
            remote(src, src, meta_send.at[slot + i], meta_recv.at[slot + i], mates[2]).wait_recv()

    for p in range(passes):
        if p > 0:
            gather_z(p)
        top_sum = bottom_sum = None
        for step in range(CHUNKS + 2):
            if step < CHUNKS:
                c = step
                for d in range(1, planes):
                    src = column.at[p, c, plane_at(-d)]
                    remote(src, src, zag_send.at[p, c, d - 1], zag_recv.at[p, c, d - 1], peers[d - 1]).wait_recv()
                rows[p, c, chip] = jnp.dot(
                    packers[p], column[p, c].reshape(count, wide), preferred_element_type=jnp.float32
                ).astype(jnp.bfloat16)
                for i, k in enumerate(order(c)):
                    src = rows.at[p, c, chip]
                    send(src, src, pag_send.at[p, c, i], pag_recv.at[p, c, i], mates[k])
            if 1 <= step <= CHUNKS:
                c = step - 1
                near, far = order(c)
                src = rows.at[p, c, mate[near]]
                remote(src, src, pag_send.at[p, c, 0], pag_recv.at[p, c, 0], mates[near]).wait_recv()
                send(src, src, pag_send.at[p, c, 2], pag_recv.at[p, c, 2], mates[far])
                if p == 0 and step == 1:
                    meta_forward()
            if step >= 2:
                c = step - 2
                near, far = order(c)
                for i, k in ((1, far), (2, 3)):
                    src = rows.at[p, c, mate[k]]
                    remote(src, src, pag_send.at[p, c, i], pag_recv.at[p, c, i], mates[far]).wait_recv()
                if p == 0 and c == 0:
                    locals_[0].wait()
                    up_copy.wait_recv()
                block = rows[p, c].reshape(CHIPS * 2 * slots, wide)
                top = jnp.dot(block, up[c * wide : (c + 1) * wide, :], preferred_element_type=jnp.float32)
                bottom = jnp.dot(
                    block, up[half + c * wide : half + (c + 1) * wide, :], preferred_element_type=jnp.float32
                )
                top_sum = top if c == 0 else top_sum + top
                bottom_sum = bottom if c == 0 else bottom_sum + bottom
        if p == 0:
            meta_finish()
            locals_[1].wait()
            down_copy.wait_recv()
        upward = (
            top_sum.reshape(CHIPS, 2, slots, 2 * HID_DEV)[:, 0]
            + bottom_sum.reshape(CHIPS, 2, slots, 2 * HID_DEV)[:, 1]
        ).reshape(CHIPS * slots, 2 * HID_DEV)
        gate = slot_gates[...].reshape(CHIPS * slots, 128)[:, p : p + 1]
        active = (upward / (1.0 + jnp.exp(-upward)) * gate).astype(jnp.bfloat16)
        for c in range(CHUNKS):
            lo, hi = c * wide, (c + 1) * wide
            top = jnp.dot(active, down[:, lo:hi], preferred_element_type=jnp.float32)
            bottom = jnp.dot(active, down[:, half + lo : half + hi], preferred_element_type=jnp.float32)
            both = jnp.concatenate(
                [top.reshape(CHIPS, slots, wide), bottom.reshape(CHIPS, slots, wide)], axis=1
            )
            part[p, c] = both.astype(jnp.bfloat16)
            near, far = order(c)
            for i, k in ((1, 3), (0, near)):
                send(
                    part.at[p, c, mate[k]], first.at[p, c, i], one_send.at[p, c, i], one_recv.at[p, c, i], mates[near]
                )
        for step in range(CHUNKS + 1):
            if step < CHUNKS:
                c = step
                near, far = order(c)
                src = first.at[p, c, 1]
                remote(src, src, one_send.at[p, c, 1], one_recv.at[p, c, 1], mates[near]).wait_recv()
                total = part[p, c, mate[far]].astype(jnp.float32) + first[p, c, 1].astype(jnp.float32)
                second_out[p, c] = total.astype(jnp.bfloat16)
                send(second_out.at[p, c], second.at[p, c], two_send.at[p, c], two_recv.at[p, c], mates[far])
            if step >= 1:
                c = step - 1
                near, far = order(c)
                src = first.at[p, c, 0]
                remote(src, src, one_send.at[p, c, 0], one_recv.at[p, c, 0], mates[near]).wait_recv()
                src = second.at[p, c]
                remote(src, src, two_send.at[p, c], two_recv.at[p, c], mates[far]).wait_recv()
                total = part[p, c, chip].astype(jnp.float32) + first[p, c, 0].astype(jnp.float32)
                total = total + second[p, c].astype(jnp.float32)
                unpacked = jnp.dot(unpackers[p], total.astype(jnp.bfloat16), preferred_element_type=jnp.float32)
                plane_sum[p, c] = unpacked.astype(jnp.bfloat16).reshape(planes, 16, wide)
                for d in range(1, planes):
                    send(
                        plane_sum.at[p, c, plane_at(d)], plane_in.at[p, c, d - 1],
                        zrs_send.at[p, c, d - 1], zrs_recv.at[p, c, d - 1], peers[d - 1],
                    )
        for c in range(CHUNKS):
            lo, hi = c * wide, (c + 1) * wide
            total = plane_sum[p, c, plane].astype(jnp.float32)
            for d in range(1, planes):
                src = plane_in.at[p, c, d - 1]
                remote(src, src, zrs_send.at[p, c, d - 1], zrs_recv.at[p, c, d - 1], peers[d - 1]).wait_recv()
                total = total + plane_in[p, c, d - 1].astype(jnp.float32)
            for h in range(2):
                value = (cur[h, :, lo:hi] + total[h * 8 : h * 8 + 8]).astype(jnp.bfloat16).astype(jnp.float32)
                cur[h, :, lo:hi] = value
        if sections > 1:
            shift_out[p] = jnp.concatenate([cur[0], cur[1]], axis=0).astype(jnp.bfloat16)
            send(shift_out.at[p], shift_in.at[p], sh_send.at[p], sh_recv.at[p], after)
            remote(shift_out.at[p], shift_in.at[p], sh_send.at[p], sh_recv.at[p], after).wait_recv()
            for h in range(2):
                cur[h] = shift_in[p].astype(jnp.float32)[h * 8 : h * 8 + 8]
    for h in range(2):
        out[:, h * half : (h + 1) * half] = cur[h].astype(jnp.bfloat16)
    up_copy.wait_send()
    down_copy.wait_send()
    for copy in pending:
        copy.wait_send()


def body(hidden, norm_gain, w_up, w_down, expert_ids, route_gates):
    width = hidden.shape[-1]
    half = width // 2
    wide = half // CHUNKS
    planes = lax.axis_size("expert") // (2 * CHIPS)
    sections = lax.axis_size("section")
    passes = expert_ids.shape[1]
    bf = jnp.bfloat16
    dma = pltpu.SemaphoreType.DMA
    away = planes - 1
    shift = passes if sections > 1 else 1
    routes = hidden.shape[1] * expert_ids.shape[-1]
    cap = min(hidden.shape[1], (routes + planes - 1) // planes + 2)
    slots = planes * cap
    vmem = pl.BlockSpec(memory_space=pltpu.VMEM)
    hbm = pl.BlockSpec(memory_space=pl.ANY)
    result = pl.pallas_call(
        functools.partial(kernel, planes, sections, passes, cap),
        out_shape=jax.ShapeDtypeStruct((8, width), bf),
        in_specs=[vmem] * 4 + [hbm] * 2,
        out_specs=vmem,
        scratch_shapes=[
            pltpu.VMEM((width, 2 * HID_DEV), bf),
            pltpu.VMEM((2 * HID_DEV, width), bf),
            pltpu.VMEM((passes, CHUNKS, planes, 16, wide), bf),
            pltpu.VMEM((passes, CHUNKS, CHIPS, 2 * slots, wide), bf),
            pltpu.VMEM((planes, 8, 128), jnp.float32),
            pltpu.VMEM((CHIPS, slots, 128), jnp.float32),
            pltpu.VMEM((passes, CHUNKS, CHIPS, 2 * slots, wide), bf),
            pltpu.VMEM((passes, CHUNKS, 2, 2 * slots, wide), bf),
            pltpu.VMEM((passes, CHUNKS, 2 * slots, wide), bf),
            pltpu.VMEM((passes, CHUNKS, 2 * slots, wide), bf),
            pltpu.VMEM((passes, CHUNKS, planes, 16, wide), bf),
            pltpu.VMEM((passes, CHUNKS, away, 16, wide), bf),
            pltpu.VMEM((2, 8, half), jnp.float32),
            pltpu.VMEM((shift, 16, half), bf),
            pltpu.VMEM((shift, 16, half), bf),
            dma((2,)), dma((2,)), dma((2,)),
            dma((away + 3,)), dma((away + 3,)),
            dma((passes, CHUNKS, away)), dma((passes, CHUNKS, away)),
            dma((passes, CHUNKS, 3)), dma((passes, CHUNKS, 3)),
            dma((passes, CHUNKS, 2)), dma((passes, CHUNKS, 2)),
            dma((passes, CHUNKS)), dma((passes, CHUNKS)),
            dma((passes, CHUNKS, away)), dma((passes, CHUNKS, away)),
            dma((shift,)), dma((shift,)),
        ],
        compiler_params=pltpu.CompilerParams(
            collective_id=0, has_side_effects=True, vmem_limit_bytes=56 * 1024 * 1024
        ),
    )(
        hidden[0], norm_gain, expert_ids[0].swapaxes(1, 2), route_gates[0].swapaxes(1, 2), w_up[0], w_down[0]
    )
    return result[None]


def solution(mesh):
    placed = (
        P("section", "expert", None),
        P("section", None),
        P("section", None, "expert"),
        P("section", "expert", None),
        P("section", None, "expert", None),
        P("section", None, "expert", None),
    )
    return jax.shard_map(
        body, mesh=mesh, in_specs=placed, out_specs=P("section", "expert", None), check_vma=False
    )
```

```python
import functools

import jax
import jax.numpy as jnp
from jax import lax
from jax.experimental import pallas as pl
from jax.experimental.pallas import tpu as pltpu
from jax.sharding import PartitionSpec as P

HID = 1024
HID_DEV = 128
CHUNKS = 4
WINDOW = 2
CHIPS = HID // HID_DEV // 2


def kernel(
    planes, sections, passes, cap,
    hidden, gain, ids, gates, up_hbm, down_hbm, out,
    up, down, column, rows, meta, slot_gates, part, first, second_out, second, plane_sum, plane_in, cur, shift_out, shift_in,
    w_local, w_send, w_recv, meta_send, meta_recv, zag_send, zag_recv, pag_send, pag_recv,
    one_send, one_recv, two_send, two_recv, zrs_send, zrs_recv, sh_send, sh_recv,
):
    me = lax.axis_index("expert")
    core = lax.rem(me, 2)
    chip = lax.rem(me // 2, CHIPS)
    plane = me // (2 * CHIPS)
    half = cur.shape[2]
    wide = half // CHUNKS
    mate = {1: chip + 1 - 2 * lax.rem(chip, 2), 2: lax.rem(chip + 2, 4), 3: 3 - chip}

    def at(plane_index, chip_index, core_index):
        return {"expert": (plane_index * CHIPS + chip_index) * 2 + core_index}

    def plane_at(by):
        return lax.rem(plane + by + planes, planes)

    partner = at(plane, chip, 1 - core)
    peers = [at(plane_at(d), chip, core) for d in range(1, planes)]
    mates = {k: at(plane, mate[k], core) for k in (1, 2)}
    targets = [partner, mates[1], mates[2]] + peers
    if sections > 1:
        sec = lax.axis_index("section")
        after = {"section": lax.rem(sec + 1, sections)}
        before = {"section": lax.rem(sec + sections - 1, sections)}
        targets = targets + [after, before]
    barrier = pltpu.get_barrier_semaphore()
    for target in targets:
        pl.semaphore_signal(barrier, inc=1, device_id=target, device_id_type=pl.DeviceIdType.MESH)
    pl.semaphore_wait(barrier, len(targets))

    pending = []

    def remote(src, dst, send, recv, target):
        return pltpu.make_async_remote_copy(
            src_ref=src, dst_ref=dst, send_sem=send, recv_sem=recv,
            device_id=target, device_id_type=pl.DeviceIdType.MESH,
        )

    def send(*args):
        copy = remote(*args)
        copy.start()
        pending.append(copy)

    lanes = lax.broadcasted_iota(jnp.int32, (8, 128), 1)
    diagonal = lax.broadcasted_iota(jnp.int32, (8, 8), 0) == lax.broadcasted_iota(jnp.int32, (8, 8), 1)
    table = jnp.zeros((8, 128), jnp.float32)
    for p in range(passes):
        for k in range(ids.shape[1]):
            named = jnp.sum(jnp.where(diagonal, ids[p, k : k + 1, :], 0).astype(jnp.float32), axis=-1, keepdims=True)
            weight = jnp.sum(jnp.where(diagonal, gates[p, k : k + 1, :], 0.0), axis=-1, keepdims=True)
            hit = lanes == named.astype(jnp.int32) + p * planes
            table = table + jnp.where(hit, weight, 0.0)
    meta[plane] = table
    for d in range(1, planes):
        send(meta.at[plane], meta.at[plane], meta_send.at[d - 1], meta_recv.at[d - 1], peers[d - 1])

    for h in range(2):
        cur[h] = hidden[:, h * half : (h + 1) * half].astype(jnp.float32)

    def gather_z(p):
        a, b = cur[0], cur[1]
        total = jnp.sum(a * a, axis=-1, keepdims=True) + jnp.sum(b * b, axis=-1, keepdims=True)
        scale = lax.rsqrt(total / (2 * half) + 1e-06)
        for c in range(CHUNKS):
            lo, hi = c * wide, (c + 1) * wide
            top = cur[0, :, lo:hi] * scale * gain[:, lo:hi]
            bottom = cur[1, :, lo:hi] * scale * gain[:, half + lo : half + hi]
            column[p, c, plane] = jnp.concatenate([top, bottom], axis=0).astype(jnp.bfloat16)
        for c in range(WINDOW):
            start_z(p, c)

    def start_z(p, c):
        block = column.at[p, c, plane]
        for d in range(1, planes):
            send(block, block, zag_send.at[p, c, d - 1], zag_recv.at[p, c, d - 1], peers[d - 1])

    def order(c):
        return (1, 2) if c % 2 == 0 else (2, 1)

    gather_z(0)
    locals_ = [
        pltpu.make_async_copy(up_hbm, up.at[:, pl.ds(0, HID_DEV)], w_local.at[0]),
        pltpu.make_async_copy(down_hbm, down.at[pl.ds(0, HID_DEV)], w_local.at[1]),
    ]
    for copy in locals_:
        copy.start()
    up_copy = remote(up_hbm, up.at[:, pl.ds(HID_DEV, HID_DEV)], w_send.at[0], w_recv.at[0], partner)
    down_copy = remote(down_hbm, down.at[pl.ds(HID_DEV, HID_DEV)], w_send.at[1], w_recv.at[1], partner)
    up_copy.start()
    down_copy.start()

    for d in range(1, planes):
        src = meta.at[plane_at(-d)]
        remote(src, src, meta_send.at[d - 1], meta_recv.at[d - 1], peers[d - 1]).wait_recv()
    slots = planes * cap
    count = planes * 16
    unpackers, packers = [], []
    gate_lanes = jnp.zeros((slots, 128), jnp.float32)
    for p in range(passes):
        pieces = []
        for g in range(planes):
            gate = jnp.sum(jnp.where(lanes == plane + p * planes, meta[g], 0.0), axis=-1, keepdims=True)
            routed = jnp.where(gate != 0.0, 1.0, 0.0)
            earlier = jnp.sum(
                jnp.where(
                    lax.broadcasted_iota(jnp.int32, (8, 8), 0) < lax.broadcasted_iota(jnp.int32, (8, 8), 1), routed, 0.0
                ),
                axis=0, keepdims=True,
            )
            place = jnp.sum(jnp.where(diagonal, earlier, 0.0), axis=-1, keepdims=True).astype(jnp.int32)
            for h in range(2):
                pieces.append(jnp.where(lanes == place + (h * slots + g * cap), gate, 0.0))
        if count < 128:
            pieces.append(jnp.zeros((128 - count, 128), jnp.float32))
        spread = jnp.concatenate(pieces, axis=0)
        turned = spread.T
        unpackers.append(jnp.where(spread[:count, : 2 * slots] != 0.0, 1.0, 0.0).astype(jnp.bfloat16))
        packers.append(jnp.where(turned[: 2 * slots, :count] != 0.0, 1.0, 0.0).astype(jnp.bfloat16))
        slot_gate = jnp.sum(turned[:slots], axis=-1, keepdims=True)
        gate_lanes = gate_lanes + jnp.where(lax.broadcasted_iota(jnp.int32, (slots, 128), 1) == p, slot_gate, 0.0)
    slot_gates[chip] = gate_lanes
    slot = planes - 1
    for i, k in enumerate((1, 2)):
        send(slot_gates.at[chip], slot_gates.at[chip], meta_send.at[slot + i], meta_recv.at[slot + i], mates[k])

    def meta_forward():
        src = slot_gates.at[mate[1]]
        remote(src, src, meta_send.at[slot], meta_recv.at[slot], mates[1]).wait_recv()
        send(src, src, meta_send.at[slot + 2], meta_recv.at[slot + 2], mates[2])

    def meta_finish():
        for i, k in ((1, 2), (2, 3)):
            src = slot_gates.at[mate[k]]
            remote(src, src, meta_send.at[slot + i], meta_recv.at[slot + i], mates[2]).wait_recv()

    for p in range(passes):
        if p > 0:
            gather_z(p)
        top_sum = bottom_sum = None
        for step in range(CHUNKS + 2):
            if step < CHUNKS:
                c = step
                for d in range(1, planes):
                    src = column.at[p, c, plane_at(-d)]
                    remote(src, src, zag_send.at[p, c, d - 1], zag_recv.at[p, c, d - 1], peers[d - 1]).wait_recv()
                if c + WINDOW < CHUNKS:
                    start_z(p, c + WINDOW)
                rows[p, c, chip] = jnp.dot(
                    packers[p], column[p, c].reshape(count, wide), preferred_element_type=jnp.float32
                ).astype(jnp.bfloat16)
                for i, k in enumerate(order(c)):
                    src = rows.at[p, c, chip]
                    send(src, src, pag_send.at[p, c, i], pag_recv.at[p, c, i], mates[k])
            if 1 <= step <= CHUNKS:
                c = step - 1
                near, far = order(c)
                src = rows.at[p, c, mate[near]]
                remote(src, src, pag_send.at[p, c, 0], pag_recv.at[p, c, 0], mates[near]).wait_recv()
                send(src, src, pag_send.at[p, c, 2], pag_recv.at[p, c, 2], mates[far])
                if p == 0 and step == 1:
                    meta_forward()
            if step >= 2:
                c = step - 2
                near, far = order(c)
                for i, k in ((1, far), (2, 3)):
                    src = rows.at[p, c, mate[k]]
                    remote(src, src, pag_send.at[p, c, i], pag_recv.at[p, c, i], mates[far]).wait_recv()
                if p == 0 and c == 0:
                    locals_[0].wait()
                    up_copy.wait_recv()
                block = rows[p, c].reshape(CHIPS * 2 * slots, wide)
                top = jnp.dot(block, up[c * wide : (c + 1) * wide, :], preferred_element_type=jnp.float32)
                bottom = jnp.dot(
                    block, up[half + c * wide : half + (c + 1) * wide, :], preferred_element_type=jnp.float32
                )
                top_sum = top if c == 0 else top_sum + top
                bottom_sum = bottom if c == 0 else bottom_sum + bottom
        if p == 0:
            meta_finish()
            locals_[1].wait()
            down_copy.wait_recv()
        upward = (
            top_sum.reshape(CHIPS, 2, slots, 2 * HID_DEV)[:, 0]
            + bottom_sum.reshape(CHIPS, 2, slots, 2 * HID_DEV)[:, 1]
        ).reshape(CHIPS * slots, 2 * HID_DEV)
        gate = slot_gates[...].reshape(CHIPS * slots, 128)[:, p : p + 1]
        active = (upward / (1.0 + jnp.exp(-upward)) * gate).astype(jnp.bfloat16)

        def start_down(c):
            lo, hi = c * wide, (c + 1) * wide
            top = jnp.dot(active, down[:, lo:hi], preferred_element_type=jnp.float32)
            bottom = jnp.dot(active, down[:, half + lo : half + hi], preferred_element_type=jnp.float32)
            both = jnp.concatenate(
                [top.reshape(CHIPS, slots, wide), bottom.reshape(CHIPS, slots, wide)], axis=1
            )
            part[p, c] = both.astype(jnp.bfloat16)
            near, far = order(c)
            for i, k in ((1, 3), (0, near)):
                send(
                    part.at[p, c, mate[k]], first.at[p, c, i], one_send.at[p, c, i], one_recv.at[p, c, i], mates[near]
                )

        for c in range(WINDOW):
            start_down(c)
        for step in range(CHUNKS + 1):
            if step < CHUNKS:
                c = step
                near, far = order(c)
                src = first.at[p, c, 1]
                remote(src, src, one_send.at[p, c, 1], one_recv.at[p, c, 1], mates[near]).wait_recv()
                total = part[p, c, mate[far]].astype(jnp.float32) + first[p, c, 1].astype(jnp.float32)
                second_out[p, c] = total.astype(jnp.bfloat16)
                send(second_out.at[p, c], second.at[p, c], two_send.at[p, c], two_recv.at[p, c], mates[far])
                if c + WINDOW < CHUNKS:
                    start_down(c + WINDOW)
            if step >= 1:
                c = step - 1
                near, far = order(c)
                src = first.at[p, c, 0]
                remote(src, src, one_send.at[p, c, 0], one_recv.at[p, c, 0], mates[near]).wait_recv()
                src = second.at[p, c]
                remote(src, src, two_send.at[p, c], two_recv.at[p, c], mates[far]).wait_recv()
                total = part[p, c, chip].astype(jnp.float32) + first[p, c, 0].astype(jnp.float32)
                total = total + second[p, c].astype(jnp.float32)
                unpacked = jnp.dot(unpackers[p], total.astype(jnp.bfloat16), preferred_element_type=jnp.float32)
                plane_sum[p, c] = unpacked.astype(jnp.bfloat16).reshape(planes, 16, wide)
                for d in range(1, planes):
                    send(
                        plane_sum.at[p, c, plane_at(d)], plane_in.at[p, c, d - 1],
                        zrs_send.at[p, c, d - 1], zrs_recv.at[p, c, d - 1], peers[d - 1],
                    )
        for c in range(CHUNKS):
            lo, hi = c * wide, (c + 1) * wide
            total = plane_sum[p, c, plane].astype(jnp.float32)
            for d in range(1, planes):
                src = plane_in.at[p, c, d - 1]
                remote(src, src, zrs_send.at[p, c, d - 1], zrs_recv.at[p, c, d - 1], peers[d - 1]).wait_recv()
                total = total + plane_in[p, c, d - 1].astype(jnp.float32)
            for h in range(2):
                value = (cur[h, :, lo:hi] + total[h * 8 : h * 8 + 8]).astype(jnp.bfloat16).astype(jnp.float32)
                cur[h, :, lo:hi] = value
        if sections > 1:
            shift_out[p] = jnp.concatenate([cur[0], cur[1]], axis=0).astype(jnp.bfloat16)
            send(shift_out.at[p], shift_in.at[p], sh_send.at[p], sh_recv.at[p], after)
            remote(shift_out.at[p], shift_in.at[p], sh_send.at[p], sh_recv.at[p], after).wait_recv()
            for h in range(2):
                cur[h] = shift_in[p].astype(jnp.float32)[h * 8 : h * 8 + 8]
    for h in range(2):
        out[:, h * half : (h + 1) * half] = cur[h].astype(jnp.bfloat16)
    up_copy.wait_send()
    down_copy.wait_send()
    for copy in pending:
        copy.wait_send()


def body(hidden, norm_gain, w_up, w_down, expert_ids, route_gates):
    width = hidden.shape[-1]
    half = width // 2
    wide = half // CHUNKS
    planes = lax.axis_size("expert") // (2 * CHIPS)
    sections = lax.axis_size("section")
    passes = expert_ids.shape[1]
    bf = jnp.bfloat16
    dma = pltpu.SemaphoreType.DMA
    away = planes - 1
    shift = passes if sections > 1 else 1
    routes = hidden.shape[1] * expert_ids.shape[-1]
    cap = min(hidden.shape[1], (routes + planes - 1) // planes + 2)
    slots = planes * cap
    vmem = pl.BlockSpec(memory_space=pltpu.VMEM)
    hbm = pl.BlockSpec(memory_space=pl.ANY)
    result = pl.pallas_call(
        functools.partial(kernel, planes, sections, passes, cap),
        out_shape=jax.ShapeDtypeStruct((8, width), bf),
        in_specs=[vmem] * 4 + [hbm] * 2,
        out_specs=vmem,
        scratch_shapes=[
            pltpu.VMEM((width, 2 * HID_DEV), bf),
            pltpu.VMEM((2 * HID_DEV, width), bf),
            pltpu.VMEM((passes, CHUNKS, planes, 16, wide), bf),
            pltpu.VMEM((passes, CHUNKS, CHIPS, 2 * slots, wide), bf),
            pltpu.VMEM((planes, 8, 128), jnp.float32),
            pltpu.VMEM((CHIPS, slots, 128), jnp.float32),
            pltpu.VMEM((passes, CHUNKS, CHIPS, 2 * slots, wide), bf),
            pltpu.VMEM((passes, CHUNKS, 2, 2 * slots, wide), bf),
            pltpu.VMEM((passes, CHUNKS, 2 * slots, wide), bf),
            pltpu.VMEM((passes, CHUNKS, 2 * slots, wide), bf),
            pltpu.VMEM((passes, CHUNKS, planes, 16, wide), bf),
            pltpu.VMEM((passes, CHUNKS, away, 16, wide), bf),
            pltpu.VMEM((2, 8, half), jnp.float32),
            pltpu.VMEM((shift, 16, half), bf),
            pltpu.VMEM((shift, 16, half), bf),
            dma((2,)), dma((2,)), dma((2,)),
            dma((away + 3,)), dma((away + 3,)),
            dma((passes, CHUNKS, away)), dma((passes, CHUNKS, away)),
            dma((passes, CHUNKS, 3)), dma((passes, CHUNKS, 3)),
            dma((passes, CHUNKS, 2)), dma((passes, CHUNKS, 2)),
            dma((passes, CHUNKS)), dma((passes, CHUNKS)),
            dma((passes, CHUNKS, away)), dma((passes, CHUNKS, away)),
            dma((shift,)), dma((shift,)),
        ],
        compiler_params=pltpu.CompilerParams(
            collective_id=0, has_side_effects=True, vmem_limit_bytes=56 * 1024 * 1024
        ),
    )(
        hidden[0], norm_gain, expert_ids[0].swapaxes(1, 2), route_gates[0].swapaxes(1, 2), w_up[0], w_down[0]
    )
    return result[None]


def solution(mesh):
    placed = (
        P("section", "expert", None),
        P("section", None),
        P("section", None, "expert"),
        P("section", "expert", None),
        P("section", None, "expert", None),
        P("section", None, "expert", None),
    )
    return jax.shard_map(
        body, mesh=mesh, in_specs=placed, out_specs=P("section", "expert", None), check_vma=False
    )
```

```python
import functools

import jax
import jax.numpy as jnp
from jax import lax
from jax.experimental import pallas as pl
from jax.experimental.pallas import tpu as pltpu
from jax.sharding import PartitionSpec as P

HID = 1024
HID_DEV = 128
CHUNKS = 4
WINDOW = 2
CHIPS = HID // HID_DEV // 2


def kernel(
    planes, sections, passes, cap,
    hidden, gain, ids, gates, up_hbm, down_hbm, out,
    up, down, column, rows, meta, slot_gates, part, first, plane_sum, plane_in, cur, shift_out, shift_in,
    w_local, w_send, w_recv, meta_send, meta_recv, zag_send, zag_recv, pag_send, pag_recv,
    one_send, one_recv, zrs_send, zrs_recv, sh_send, sh_recv,
):
    me = lax.axis_index("expert")
    core = lax.rem(me, 2)
    chip = lax.rem(me // 2, CHIPS)
    plane = me // (2 * CHIPS)
    half = cur.shape[2]
    wide = half // CHUNKS
    mate = {1: chip + 1 - 2 * lax.rem(chip, 2), 2: lax.rem(chip + 2, 4), 3: 3 - chip}

    def at(plane_index, chip_index, core_index):
        return {"expert": (plane_index * CHIPS + chip_index) * 2 + core_index}

    def plane_at(by):
        return lax.rem(plane + by + planes, planes)

    partner = at(plane, chip, 1 - core)
    peers = [at(plane_at(d), chip, core) for d in range(1, planes)]
    mates = {k: at(plane, mate[k], core) for k in (1, 2, 3)}
    targets = [partner, mates[1], mates[2], mates[3]] + peers
    if sections > 1:
        sec = lax.axis_index("section")
        after = {"section": lax.rem(sec + 1, sections)}
        before = {"section": lax.rem(sec + sections - 1, sections)}
        targets = targets + [after, before]
    barrier = pltpu.get_barrier_semaphore()
    for target in targets:
        pl.semaphore_signal(barrier, inc=1, device_id=target, device_id_type=pl.DeviceIdType.MESH)
    pl.semaphore_wait(barrier, len(targets))

    pending = []

    def remote(src, dst, send, recv, target):
        return pltpu.make_async_remote_copy(
            src_ref=src, dst_ref=dst, send_sem=send, recv_sem=recv,
            device_id=target, device_id_type=pl.DeviceIdType.MESH,
        )

    def send(*args):
        copy = remote(*args)
        copy.start()
        pending.append(copy)

    lanes = lax.broadcasted_iota(jnp.int32, (8, 128), 1)
    diagonal = lax.broadcasted_iota(jnp.int32, (8, 8), 0) == lax.broadcasted_iota(jnp.int32, (8, 8), 1)
    table = jnp.zeros((8, 128), jnp.float32)
    for p in range(passes):
        for k in range(ids.shape[1]):
            named = jnp.sum(jnp.where(diagonal, ids[p, k : k + 1, :], 0).astype(jnp.float32), axis=-1, keepdims=True)
            weight = jnp.sum(jnp.where(diagonal, gates[p, k : k + 1, :], 0.0), axis=-1, keepdims=True)
            hit = lanes == named.astype(jnp.int32) + p * planes
            table = table + jnp.where(hit, weight, 0.0)
    meta[plane] = table
    for d in range(1, planes):
        send(meta.at[plane], meta.at[plane], meta_send.at[d - 1], meta_recv.at[d - 1], peers[d - 1])

    for h in range(2):
        cur[h] = hidden[:, h * half : (h + 1) * half].astype(jnp.float32)

    def gather_z(p):
        a, b = cur[0], cur[1]
        total = jnp.sum(a * a, axis=-1, keepdims=True) + jnp.sum(b * b, axis=-1, keepdims=True)
        scale = lax.rsqrt(total / (2 * half) + 1e-06)
        for c in range(CHUNKS):
            lo, hi = c * wide, (c + 1) * wide
            top = cur[0, :, lo:hi] * scale * gain[:, lo:hi]
            bottom = cur[1, :, lo:hi] * scale * gain[:, half + lo : half + hi]
            column[p, c, plane] = jnp.concatenate([top, bottom], axis=0).astype(jnp.bfloat16)
        for c in range(WINDOW):
            start_z(p, c)

    def start_z(p, c):
        block = column.at[p, c, plane]
        for d in range(1, planes):
            send(block, block, zag_send.at[p, c, d - 1], zag_recv.at[p, c, d - 1], peers[d - 1])

    gather_z(0)
    locals_ = [
        pltpu.make_async_copy(up_hbm, up.at[:, pl.ds(0, HID_DEV)], w_local.at[0]),
        pltpu.make_async_copy(down_hbm, down.at[pl.ds(0, HID_DEV)], w_local.at[1]),
    ]
    for copy in locals_:
        copy.start()
    up_copy = remote(up_hbm, up.at[:, pl.ds(HID_DEV, HID_DEV)], w_send.at[0], w_recv.at[0], partner)
    down_copy = remote(down_hbm, down.at[pl.ds(HID_DEV, HID_DEV)], w_send.at[1], w_recv.at[1], partner)
    up_copy.start()
    down_copy.start()

    for d in range(1, planes):
        src = meta.at[plane_at(-d)]
        remote(src, src, meta_send.at[d - 1], meta_recv.at[d - 1], peers[d - 1]).wait_recv()
    slots = planes * cap
    count = planes * 16
    unpackers, packers = [], []
    gate_lanes = jnp.zeros((slots, 128), jnp.float32)
    for p in range(passes):
        pieces = []
        for g in range(planes):
            gate = jnp.sum(jnp.where(lanes == plane + p * planes, meta[g], 0.0), axis=-1, keepdims=True)
            routed = jnp.where(gate != 0.0, 1.0, 0.0)
            earlier = jnp.sum(
                jnp.where(
                    lax.broadcasted_iota(jnp.int32, (8, 8), 0) < lax.broadcasted_iota(jnp.int32, (8, 8), 1), routed, 0.0
                ),
                axis=0, keepdims=True,
            )
            place = jnp.sum(jnp.where(diagonal, earlier, 0.0), axis=-1, keepdims=True).astype(jnp.int32)
            for h in range(2):
                pieces.append(jnp.where(lanes == place + (h * slots + g * cap), gate, 0.0))
        if count < 128:
            pieces.append(jnp.zeros((128 - count, 128), jnp.float32))
        spread = jnp.concatenate(pieces, axis=0)
        turned = spread.T
        unpackers.append(jnp.where(spread[:count, : 2 * slots] != 0.0, 1.0, 0.0).astype(jnp.bfloat16))
        packers.append(jnp.where(turned[: 2 * slots, :count] != 0.0, 1.0, 0.0).astype(jnp.bfloat16))
        slot_gate = jnp.sum(turned[:slots], axis=-1, keepdims=True)
        gate_lanes = gate_lanes + jnp.where(lax.broadcasted_iota(jnp.int32, (slots, 128), 1) == p, slot_gate, 0.0)
    slot_gates[chip] = gate_lanes
    slot = planes - 1
    for k in (3, 1, 2):
        src = slot_gates.at[chip]
        send(src, src, meta_send.at[slot + k - 1], meta_recv.at[slot + k - 1], mates[k])

    def meta_finish():
        for k in (1, 2, 3):
            src = slot_gates.at[mate[k]]
            remote(src, src, meta_send.at[slot + k - 1], meta_recv.at[slot + k - 1], mates[k]).wait_recv()

    for p in range(passes):
        if p > 0:
            gather_z(p)
        top_sum = bottom_sum = None
        for step in range(CHUNKS + 1):
            if step < CHUNKS:
                c = step
                for d in range(1, planes):
                    src = column.at[p, c, plane_at(-d)]
                    remote(src, src, zag_send.at[p, c, d - 1], zag_recv.at[p, c, d - 1], peers[d - 1]).wait_recv()
                if c + WINDOW < CHUNKS:
                    start_z(p, c + WINDOW)
                rows[p, c, chip] = jnp.dot(
                    packers[p], column[p, c].reshape(count, wide), preferred_element_type=jnp.float32
                ).astype(jnp.bfloat16)
                for k in (3, 1, 2):
                    src = rows.at[p, c, chip]
                    send(src, src, pag_send.at[p, c, k - 1], pag_recv.at[p, c, k - 1], mates[k])
            if step >= 1:
                c = step - 1
                for k in (1, 2, 3):
                    src = rows.at[p, c, mate[k]]
                    remote(src, src, pag_send.at[p, c, k - 1], pag_recv.at[p, c, k - 1], mates[k]).wait_recv()
                if p == 0 and c == 0:
                    locals_[0].wait()
                    up_copy.wait_recv()
                block = rows[p, c].reshape(CHIPS * 2 * slots, wide)
                top = jnp.dot(block, up[c * wide : (c + 1) * wide, :], preferred_element_type=jnp.float32)
                bottom = jnp.dot(
                    block, up[half + c * wide : half + (c + 1) * wide, :], preferred_element_type=jnp.float32
                )
                top_sum = top if c == 0 else top_sum + top
                bottom_sum = bottom if c == 0 else bottom_sum + bottom
        if p == 0:
            meta_finish()
            locals_[1].wait()
            down_copy.wait_recv()
        upward = (
            top_sum.reshape(CHIPS, 2, slots, 2 * HID_DEV)[:, 0]
            + bottom_sum.reshape(CHIPS, 2, slots, 2 * HID_DEV)[:, 1]
        ).reshape(CHIPS * slots, 2 * HID_DEV)
        gate = slot_gates[...].reshape(CHIPS * slots, 128)[:, p : p + 1]
        active = (upward / (1.0 + jnp.exp(-upward)) * gate).astype(jnp.bfloat16)

        def start_down(c):
            lo, hi = c * wide, (c + 1) * wide
            top = jnp.dot(active, down[:, lo:hi], preferred_element_type=jnp.float32)
            bottom = jnp.dot(active, down[:, half + lo : half + hi], preferred_element_type=jnp.float32)
            both = jnp.concatenate(
                [top.reshape(CHIPS, slots, wide), bottom.reshape(CHIPS, slots, wide)], axis=1
            )
            part[p, c] = both.astype(jnp.bfloat16)
            for k in (3, 1, 2):
                send(
                    part.at[p, c, mate[k]], first.at[p, c, k - 1],
                    one_send.at[p, c, k - 1], one_recv.at[p, c, k - 1], mates[k],
                )

        for c in range(WINDOW):
            start_down(c)
        for c in range(CHUNKS):
            total = part[p, c, chip].astype(jnp.float32)
            for k in (1, 2, 3):
                src = first.at[p, c, k - 1]
                remote(src, src, one_send.at[p, c, k - 1], one_recv.at[p, c, k - 1], mates[k]).wait_recv()
                total = total + first[p, c, k - 1].astype(jnp.float32)
            if c + WINDOW < CHUNKS:
                start_down(c + WINDOW)
            unpacked = jnp.dot(unpackers[p], total.astype(jnp.bfloat16), preferred_element_type=jnp.float32)
            plane_sum[p, c] = unpacked.astype(jnp.bfloat16).reshape(planes, 16, wide)
            for d in range(1, planes):
                send(
                    plane_sum.at[p, c, plane_at(d)], plane_in.at[p, c, d - 1],
                    zrs_send.at[p, c, d - 1], zrs_recv.at[p, c, d - 1], peers[d - 1],
                )
        for c in range(CHUNKS):
            lo, hi = c * wide, (c + 1) * wide
            total = plane_sum[p, c, plane].astype(jnp.float32)
            for d in range(1, planes):
                src = plane_in.at[p, c, d - 1]
                remote(src, src, zrs_send.at[p, c, d - 1], zrs_recv.at[p, c, d - 1], peers[d - 1]).wait_recv()
                total = total + plane_in[p, c, d - 1].astype(jnp.float32)
            for h in range(2):
                value = (cur[h, :, lo:hi] + total[h * 8 : h * 8 + 8]).astype(jnp.bfloat16).astype(jnp.float32)
                cur[h, :, lo:hi] = value
        if sections > 1:
            shift_out[p] = jnp.concatenate([cur[0], cur[1]], axis=0).astype(jnp.bfloat16)
            send(shift_out.at[p], shift_in.at[p], sh_send.at[p], sh_recv.at[p], after)
            remote(shift_out.at[p], shift_in.at[p], sh_send.at[p], sh_recv.at[p], after).wait_recv()
            for h in range(2):
                cur[h] = shift_in[p].astype(jnp.float32)[h * 8 : h * 8 + 8]
    for h in range(2):
        out[:, h * half : (h + 1) * half] = cur[h].astype(jnp.bfloat16)
    up_copy.wait_send()
    down_copy.wait_send()
    for copy in pending:
        copy.wait_send()


def body(hidden, norm_gain, w_up, w_down, expert_ids, route_gates):
    width = hidden.shape[-1]
    half = width // 2
    wide = half // CHUNKS
    planes = lax.axis_size("expert") // (2 * CHIPS)
    sections = lax.axis_size("section")
    passes = expert_ids.shape[1]
    bf = jnp.bfloat16
    dma = pltpu.SemaphoreType.DMA
    away = planes - 1
    shift = passes if sections > 1 else 1
    routes = hidden.shape[1] * expert_ids.shape[-1]
    cap = min(hidden.shape[1], (routes + planes - 1) // planes + 2)
    slots = planes * cap
    vmem = pl.BlockSpec(memory_space=pltpu.VMEM)
    hbm = pl.BlockSpec(memory_space=pl.ANY)
    result = pl.pallas_call(
        functools.partial(kernel, planes, sections, passes, cap),
        out_shape=jax.ShapeDtypeStruct((8, width), bf),
        in_specs=[vmem] * 4 + [hbm] * 2,
        out_specs=vmem,
        scratch_shapes=[
            pltpu.VMEM((width, 2 * HID_DEV), bf),
            pltpu.VMEM((2 * HID_DEV, width), bf),
            pltpu.VMEM((passes, CHUNKS, planes, 16, wide), bf),
            pltpu.VMEM((passes, CHUNKS, CHIPS, 2 * slots, wide), bf),
            pltpu.VMEM((planes, 8, 128), jnp.float32),
            pltpu.VMEM((CHIPS, slots, 128), jnp.float32),
            pltpu.VMEM((passes, CHUNKS, CHIPS, 2 * slots, wide), bf),
            pltpu.VMEM((passes, CHUNKS, 3, 2 * slots, wide), bf),
            pltpu.VMEM((passes, CHUNKS, planes, 16, wide), bf),
            pltpu.VMEM((passes, CHUNKS, away, 16, wide), bf),
            pltpu.VMEM((2, 8, half), jnp.float32),
            pltpu.VMEM((shift, 16, half), bf),
            pltpu.VMEM((shift, 16, half), bf),
            dma((2,)), dma((2,)), dma((2,)),
            dma((away + 3,)), dma((away + 3,)),
            dma((passes, CHUNKS, away)), dma((passes, CHUNKS, away)),
            dma((passes, CHUNKS, 3)), dma((passes, CHUNKS, 3)),
            dma((passes, CHUNKS, 3)), dma((passes, CHUNKS, 3)),
            dma((passes, CHUNKS, away)), dma((passes, CHUNKS, away)),
            dma((shift,)), dma((shift,)),
        ],
        compiler_params=pltpu.CompilerParams(
            collective_id=0, has_side_effects=True, vmem_limit_bytes=56 * 1024 * 1024
        ),
    )(
        hidden[0], norm_gain, expert_ids[0].swapaxes(1, 2), route_gates[0].swapaxes(1, 2), w_up[0], w_down[0]
    )
    return result[None]


def solution(mesh):
    placed = (
        P("section", "expert", None),
        P("section", None),
        P("section", None, "expert"),
        P("section", "expert", None),
        P("section", None, "expert", None),
        P("section", None, "expert", None),
    )
    return jax.shard_map(
        body, mesh=mesh, in_specs=placed, out_specs=P("section", "expert", None), check_vma=False
    )
```

```python
import functools

import jax
import jax.numpy as jnp
from jax import lax
from jax.experimental import pallas as pl
from jax.experimental.pallas import tpu as pltpu
from jax.sharding import PartitionSpec as P

HID = 1024
HID_DEV = 128
CHUNKS = 7
WINDOW = 3
CHIPS = HID // HID_DEV // 2


def kernel(
    planes, sections, passes, cap,
    hidden, gain, ids, gates, up_hbm, down_hbm, out,
    up, down, column, rows, meta, slot_gates, part, first, plane_sum, plane_in, cur, shift_out, shift_in,
    w_local, w_send, w_recv, meta_send, meta_recv, zag_send, zag_recv, pag_send, pag_recv,
    one_send, one_recv, zrs_send, zrs_recv, sh_send, sh_recv,
):
    me = lax.axis_index("expert")
    core = lax.rem(me, 2)
    chip = lax.rem(me // 2, CHIPS)
    plane = me // (2 * CHIPS)
    half = cur.shape[2]
    wide = half // CHUNKS
    mate = {1: chip + 1 - 2 * lax.rem(chip, 2), 2: lax.rem(chip + 2, 4), 3: 3 - chip}

    def at(plane_index, chip_index, core_index):
        return {"expert": (plane_index * CHIPS + chip_index) * 2 + core_index}

    def plane_at(by):
        return lax.rem(plane + by + planes, planes)

    partner = at(plane, chip, 1 - core)
    peers = [at(plane_at(d), chip, core) for d in range(1, planes)]
    mates = {k: at(plane, mate[k], core) for k in (1, 2, 3)}
    targets = [partner, mates[1], mates[2], mates[3]] + peers
    if sections > 1:
        sec = lax.axis_index("section")
        after = {"section": lax.rem(sec + 1, sections)}
        before = {"section": lax.rem(sec + sections - 1, sections)}
        targets = targets + [after, before]
    barrier = pltpu.get_barrier_semaphore()
    for target in targets:
        pl.semaphore_signal(barrier, inc=1, device_id=target, device_id_type=pl.DeviceIdType.MESH)
    pl.semaphore_wait(barrier, len(targets))

    pending = []

    def remote(src, dst, send, recv, target):
        return pltpu.make_async_remote_copy(
            src_ref=src, dst_ref=dst, send_sem=send, recv_sem=recv,
            device_id=target, device_id_type=pl.DeviceIdType.MESH,
        )

    def send(*args):
        copy = remote(*args)
        copy.start()
        pending.append(copy)

    lanes = lax.broadcasted_iota(jnp.int32, (8, 128), 1)
    diagonal = lax.broadcasted_iota(jnp.int32, (8, 8), 0) == lax.broadcasted_iota(jnp.int32, (8, 8), 1)
    table = jnp.zeros((8, 128), jnp.float32)
    for p in range(passes):
        for k in range(ids.shape[1]):
            named = jnp.sum(jnp.where(diagonal, ids[p, k : k + 1, :], 0).astype(jnp.float32), axis=-1, keepdims=True)
            weight = jnp.sum(jnp.where(diagonal, gates[p, k : k + 1, :], 0.0), axis=-1, keepdims=True)
            hit = lanes == named.astype(jnp.int32) + p * planes
            table = table + jnp.where(hit, weight, 0.0)
    meta[plane] = table
    for d in range(1, planes):
        send(meta.at[plane], meta.at[plane], meta_send.at[d - 1], meta_recv.at[d - 1], peers[d - 1])

    for h in range(2):
        cur[h] = hidden[:, h * half : (h + 1) * half].astype(jnp.float32)

    def gather_z(p):
        a, b = cur[0], cur[1]
        total = jnp.sum(a * a, axis=-1, keepdims=True) + jnp.sum(b * b, axis=-1, keepdims=True)
        scale = lax.rsqrt(total / (2 * half) + 1e-06)
        for c in range(CHUNKS):
            lo, hi = c * wide, (c + 1) * wide
            top = cur[0, :, lo:hi] * scale * gain[:, lo:hi]
            bottom = cur[1, :, lo:hi] * scale * gain[:, half + lo : half + hi]
            column[p, c, plane] = jnp.concatenate([top, bottom], axis=0).astype(jnp.bfloat16)
        for c in range(WINDOW):
            start_z(p, c)

    def start_z(p, c):
        block = column.at[p, c, plane]
        for d in range(1, planes):
            send(block, block, zag_send.at[p, c, d - 1], zag_recv.at[p, c, d - 1], peers[d - 1])

    gather_z(0)
    locals_ = [
        pltpu.make_async_copy(up_hbm, up.at[:, pl.ds(0, HID_DEV)], w_local.at[0]),
        pltpu.make_async_copy(down_hbm, down.at[pl.ds(0, HID_DEV)], w_local.at[1]),
    ]
    for copy in locals_:
        copy.start()
    up_copy = remote(up_hbm, up.at[:, pl.ds(HID_DEV, HID_DEV)], w_send.at[0], w_recv.at[0], partner)
    down_copy = remote(down_hbm, down.at[pl.ds(HID_DEV, HID_DEV)], w_send.at[1], w_recv.at[1], partner)
    up_copy.start()
    down_copy.start()

    for d in range(1, planes):
        src = meta.at[plane_at(-d)]
        remote(src, src, meta_send.at[d - 1], meta_recv.at[d - 1], peers[d - 1]).wait_recv()
    slots = planes * cap
    count = planes * 16
    unpackers, packers = [], []
    gate_lanes = jnp.zeros((slots, 128), jnp.float32)
    for p in range(passes):
        pieces = []
        for g in range(planes):
            gate = jnp.sum(jnp.where(lanes == plane + p * planes, meta[g], 0.0), axis=-1, keepdims=True)
            routed = jnp.where(gate != 0.0, 1.0, 0.0)
            earlier = jnp.sum(
                jnp.where(
                    lax.broadcasted_iota(jnp.int32, (8, 8), 0) < lax.broadcasted_iota(jnp.int32, (8, 8), 1), routed, 0.0
                ),
                axis=0, keepdims=True,
            )
            place = jnp.sum(jnp.where(diagonal, earlier, 0.0), axis=-1, keepdims=True).astype(jnp.int32)
            for h in range(2):
                pieces.append(jnp.where(lanes == place + (h * slots + g * cap), gate, 0.0))
        if count < 128:
            pieces.append(jnp.zeros((128 - count, 128), jnp.float32))
        spread = jnp.concatenate(pieces, axis=0)
        turned = spread.T
        unpackers.append(jnp.where(spread[:count, : 2 * slots] != 0.0, 1.0, 0.0).astype(jnp.bfloat16))
        packers.append(jnp.where(turned[: 2 * slots, :count] != 0.0, 1.0, 0.0).astype(jnp.bfloat16))
        slot_gate = jnp.sum(turned[:slots], axis=-1, keepdims=True)
        gate_lanes = gate_lanes + jnp.where(lax.broadcasted_iota(jnp.int32, (slots, 128), 1) == p, slot_gate, 0.0)
    slot_gates[chip] = gate_lanes
    slot = planes - 1
    for k in (3, 1, 2):
        src = slot_gates.at[chip]
        send(src, src, meta_send.at[slot + k - 1], meta_recv.at[slot + k - 1], mates[k])

    def meta_finish():
        for k in (1, 2, 3):
            src = slot_gates.at[mate[k]]
            remote(src, src, meta_send.at[slot + k - 1], meta_recv.at[slot + k - 1], mates[k]).wait_recv()

    for p in range(passes):
        if p > 0:
            gather_z(p)
        top_sum = bottom_sum = None
        for step in range(CHUNKS + 1):
            if step < CHUNKS:
                c = step
                for d in range(1, planes):
                    src = column.at[p, c, plane_at(-d)]
                    remote(src, src, zag_send.at[p, c, d - 1], zag_recv.at[p, c, d - 1], peers[d - 1]).wait_recv()
                if c + WINDOW < CHUNKS:
                    start_z(p, c + WINDOW)
                rows[p, c, chip] = jnp.dot(
                    packers[p], column[p, c].reshape(count, wide), preferred_element_type=jnp.float32
                ).astype(jnp.bfloat16)
                for k in (3, 1, 2):
                    src = rows.at[p, c, chip]
                    send(src, src, pag_send.at[p, c, k - 1], pag_recv.at[p, c, k - 1], mates[k])
            if step >= 1:
                c = step - 1
                for k in (1, 2, 3):
                    src = rows.at[p, c, mate[k]]
                    remote(src, src, pag_send.at[p, c, k - 1], pag_recv.at[p, c, k - 1], mates[k]).wait_recv()
                if p == 0 and c == 0:
                    locals_[0].wait()
                    up_copy.wait_recv()
                block = rows[p, c].reshape(CHIPS * 2 * slots, wide)
                top = jnp.dot(block, up[c * wide : (c + 1) * wide, :], preferred_element_type=jnp.float32)
                bottom = jnp.dot(
                    block, up[half + c * wide : half + (c + 1) * wide, :], preferred_element_type=jnp.float32
                )
                top_sum = top if c == 0 else top_sum + top
                bottom_sum = bottom if c == 0 else bottom_sum + bottom
        if p == 0:
            meta_finish()
            locals_[1].wait()
            down_copy.wait_recv()
        upward = (
            top_sum.reshape(CHIPS, 2, slots, 2 * HID_DEV)[:, 0]
            + bottom_sum.reshape(CHIPS, 2, slots, 2 * HID_DEV)[:, 1]
        ).reshape(CHIPS * slots, 2 * HID_DEV)
        gate = slot_gates[...].reshape(CHIPS * slots, 128)[:, p : p + 1]
        active = (upward / (1.0 + jnp.exp(-upward)) * gate).astype(jnp.bfloat16)

        def start_down(c):
            lo, hi = c * wide, (c + 1) * wide
            top = jnp.dot(active, down[:, lo:hi], preferred_element_type=jnp.float32)
            bottom = jnp.dot(active, down[:, half + lo : half + hi], preferred_element_type=jnp.float32)
            both = jnp.concatenate(
                [top.reshape(CHIPS, slots, wide), bottom.reshape(CHIPS, slots, wide)], axis=1
            )
            part[p, c] = both.astype(jnp.bfloat16)
            for k in (3, 1, 2):
                send(
                    part.at[p, c, mate[k]], first.at[p, c, k - 1],
                    one_send.at[p, c, k - 1], one_recv.at[p, c, k - 1], mates[k],
                )

        for c in range(WINDOW):
            start_down(c)
        for c in range(CHUNKS):
            total = part[p, c, chip].astype(jnp.float32)
            for k in (1, 2, 3):
                src = first.at[p, c, k - 1]
                remote(src, src, one_send.at[p, c, k - 1], one_recv.at[p, c, k - 1], mates[k]).wait_recv()
                total = total + first[p, c, k - 1].astype(jnp.float32)
            if c + WINDOW < CHUNKS:
                start_down(c + WINDOW)
            unpacked = jnp.dot(unpackers[p], total.astype(jnp.bfloat16), preferred_element_type=jnp.float32)
            plane_sum[p, c] = unpacked.astype(jnp.bfloat16).reshape(planes, 16, wide)
            for d in range(1, planes):
                send(
                    plane_sum.at[p, c, plane_at(d)], plane_in.at[p, c, d - 1],
                    zrs_send.at[p, c, d - 1], zrs_recv.at[p, c, d - 1], peers[d - 1],
                )
        for c in range(CHUNKS):
            lo, hi = c * wide, (c + 1) * wide
            total = plane_sum[p, c, plane].astype(jnp.float32)
            for d in range(1, planes):
                src = plane_in.at[p, c, d - 1]
                remote(src, src, zrs_send.at[p, c, d - 1], zrs_recv.at[p, c, d - 1], peers[d - 1]).wait_recv()
                total = total + plane_in[p, c, d - 1].astype(jnp.float32)
            for h in range(2):
                value = (cur[h, :, lo:hi] + total[h * 8 : h * 8 + 8]).astype(jnp.bfloat16).astype(jnp.float32)
                cur[h, :, lo:hi] = value
        if sections > 1:
            shift_out[p] = jnp.concatenate([cur[0], cur[1]], axis=0).astype(jnp.bfloat16)
            send(shift_out.at[p], shift_in.at[p], sh_send.at[p], sh_recv.at[p], after)
            remote(shift_out.at[p], shift_in.at[p], sh_send.at[p], sh_recv.at[p], after).wait_recv()
            for h in range(2):
                cur[h] = shift_in[p].astype(jnp.float32)[h * 8 : h * 8 + 8]
    for h in range(2):
        out[:, h * half : (h + 1) * half] = cur[h].astype(jnp.bfloat16)
    up_copy.wait_send()
    down_copy.wait_send()
    for copy in pending:
        copy.wait_send()


def body(hidden, norm_gain, w_up, w_down, expert_ids, route_gates):
    width = hidden.shape[-1]
    half = width // 2
    wide = half // CHUNKS
    planes = lax.axis_size("expert") // (2 * CHIPS)
    sections = lax.axis_size("section")
    passes = expert_ids.shape[1]
    bf = jnp.bfloat16
    dma = pltpu.SemaphoreType.DMA
    away = planes - 1
    shift = passes if sections > 1 else 1
    routes = hidden.shape[1] * expert_ids.shape[-1]
    cap = min(hidden.shape[1], (routes + planes - 1) // planes + 2)
    slots = planes * cap
    vmem = pl.BlockSpec(memory_space=pltpu.VMEM)
    hbm = pl.BlockSpec(memory_space=pl.ANY)
    result = pl.pallas_call(
        functools.partial(kernel, planes, sections, passes, cap),
        out_shape=jax.ShapeDtypeStruct((8, width), bf),
        in_specs=[vmem] * 4 + [hbm] * 2,
        out_specs=vmem,
        scratch_shapes=[
            pltpu.VMEM((width, 2 * HID_DEV), bf),
            pltpu.VMEM((2 * HID_DEV, width), bf),
            pltpu.VMEM((passes, CHUNKS, planes, 16, wide), bf),
            pltpu.VMEM((passes, CHUNKS, CHIPS, 2 * slots, wide), bf),
            pltpu.VMEM((planes, 8, 128), jnp.float32),
            pltpu.VMEM((CHIPS, slots, 128), jnp.float32),
            pltpu.VMEM((passes, CHUNKS, CHIPS, 2 * slots, wide), bf),
            pltpu.VMEM((passes, CHUNKS, 3, 2 * slots, wide), bf),
            pltpu.VMEM((passes, CHUNKS, planes, 16, wide), bf),
            pltpu.VMEM((passes, CHUNKS, away, 16, wide), bf),
            pltpu.VMEM((2, 8, half), jnp.float32),
            pltpu.VMEM((shift, 16, half), bf),
            pltpu.VMEM((shift, 16, half), bf),
            dma((2,)), dma((2,)), dma((2,)),
            dma((away + 3,)), dma((away + 3,)),
            dma((passes, CHUNKS, away)), dma((passes, CHUNKS, away)),
            dma((passes, CHUNKS, 3)), dma((passes, CHUNKS, 3)),
            dma((passes, CHUNKS, 3)), dma((passes, CHUNKS, 3)),
            dma((passes, CHUNKS, away)), dma((passes, CHUNKS, away)),
            dma((shift,)), dma((shift,)),
        ],
        compiler_params=pltpu.CompilerParams(
            collective_id=0, has_side_effects=True, vmem_limit_bytes=56 * 1024 * 1024
        ),
    )(
        hidden[0], norm_gain, expert_ids[0].swapaxes(1, 2), route_gates[0].swapaxes(1, 2), w_up[0], w_down[0]
    )
    return result[None]


def solution(mesh):
    placed = (
        P("section", "expert", None),
        P("section", None),
        P("section", None, "expert"),
        P("section", "expert", None),
        P("section", None, "expert", None),
        P("section", None, "expert", None),
    )
    return jax.shard_map(
        body, mesh=mesh, in_specs=placed, out_specs=P("section", "expert", None), check_vma=False
    )
```

```python
import functools

import jax
import jax.numpy as jnp
from jax import lax
from jax.experimental import pallas as pl
from jax.experimental.pallas import tpu as pltpu
from jax.sharding import PartitionSpec as P

HID = 1024
HID_DEV = 128
CHUNKS = 2
WINDOW = 2
CHIPS = HID // HID_DEV // 2


def kernel(
    planes, sections, passes, cap,
    hidden, gain, ids, gates, up_hbm, down_hbm, out,
    up, down, column, rows, meta, slot_gates, part, first, plane_sum, plane_in, cur, shift_out, shift_in,
    w_local, w_send, w_recv, meta_send, meta_recv, zag_send, zag_recv, pag_send, pag_recv,
    one_send, one_recv, zrs_send, zrs_recv, sh_send, sh_recv,
):
    me = lax.axis_index("expert")
    core = lax.rem(me, 2)
    chip = lax.rem(me // 2, CHIPS)
    plane = me // (2 * CHIPS)
    half = cur.shape[2]
    wide = half // CHUNKS
    mate = {1: chip + 1 - 2 * lax.rem(chip, 2), 2: lax.rem(chip + 2, 4), 3: 3 - chip}

    def at(plane_index, chip_index, core_index):
        return {"expert": (plane_index * CHIPS + chip_index) * 2 + core_index}

    def plane_at(by):
        return lax.rem(plane + by + planes, planes)

    partner = at(plane, chip, 1 - core)
    peers = [at(plane_at(d), chip, core) for d in range(1, planes)]
    mates = {k: at(plane, mate[k], core) for k in (1, 2, 3)}
    targets = [partner, mates[1], mates[2], mates[3]] + peers
    if sections > 1:
        sec = lax.axis_index("section")
        after = {"section": lax.rem(sec + 1, sections)}
        before = {"section": lax.rem(sec + sections - 1, sections)}
        targets = targets + [after, before]
    barrier = pltpu.get_barrier_semaphore()
    for target in targets:
        pl.semaphore_signal(barrier, inc=1, device_id=target, device_id_type=pl.DeviceIdType.MESH)
    pl.semaphore_wait(barrier, len(targets))

    pending = []

    def remote(src, dst, send, recv, target):
        return pltpu.make_async_remote_copy(
            src_ref=src, dst_ref=dst, send_sem=send, recv_sem=recv,
            device_id=target, device_id_type=pl.DeviceIdType.MESH,
        )

    def send(*args):
        copy = remote(*args)
        copy.start()
        pending.append(copy)

    lanes = lax.broadcasted_iota(jnp.int32, (8, 128), 1)
    diagonal = lax.broadcasted_iota(jnp.int32, (8, 8), 0) == lax.broadcasted_iota(jnp.int32, (8, 8), 1)
    table = jnp.zeros((8, 128), jnp.float32)
    for p in range(passes):
        for k in range(ids.shape[1]):
            named = jnp.sum(jnp.where(diagonal, ids[p, k : k + 1, :], 0).astype(jnp.float32), axis=-1, keepdims=True)
            weight = jnp.sum(jnp.where(diagonal, gates[p, k : k + 1, :], 0.0), axis=-1, keepdims=True)
            hit = lanes == named.astype(jnp.int32) + p * planes
            table = table + jnp.where(hit, weight, 0.0)
    meta[plane] = table
    for d in range(1, planes):
        send(meta.at[plane], meta.at[plane], meta_send.at[d - 1], meta_recv.at[d - 1], peers[d - 1])

    for h in range(2):
        cur[h] = hidden[:, h * half : (h + 1) * half].astype(jnp.float32)

    def gather_z(p):
        a, b = cur[0], cur[1]
        total = jnp.sum(a * a, axis=-1, keepdims=True) + jnp.sum(b * b, axis=-1, keepdims=True)
        scale = lax.rsqrt(total / (2 * half) + 1e-06)
        for c in range(CHUNKS):
            lo, hi = c * wide, (c + 1) * wide
            top = cur[0, :, lo:hi] * scale * gain[:, lo:hi]
            bottom = cur[1, :, lo:hi] * scale * gain[:, half + lo : half + hi]
            column[p, c, plane] = jnp.concatenate([top, bottom], axis=0).astype(jnp.bfloat16)
        for c in range(WINDOW):
            start_z(p, c)

    def start_z(p, c):
        block = column.at[p, c, plane]
        for d in range(1, planes):
            send(block, block, zag_send.at[p, c, d - 1], zag_recv.at[p, c, d - 1], peers[d - 1])

    locals_ = [
        pltpu.make_async_copy(up_hbm, up.at[:, pl.ds(0, HID_DEV)], w_local.at[0]),
        pltpu.make_async_copy(down_hbm, down.at[pl.ds(0, HID_DEV)], w_local.at[1]),
    ]
    for copy in locals_:
        copy.start()
    up_copy = remote(up_hbm, up.at[:, pl.ds(HID_DEV, HID_DEV)], w_send.at[0], w_recv.at[0], partner)
    down_copy = remote(down_hbm, down.at[pl.ds(HID_DEV, HID_DEV)], w_send.at[1], w_recv.at[1], partner)
    up_copy.start()
    gather_z(0)
    down_copy.start()

    for d in range(1, planes):
        src = meta.at[plane_at(-d)]
        remote(src, src, meta_send.at[d - 1], meta_recv.at[d - 1], peers[d - 1]).wait_recv()
    slots = planes * cap
    count = planes * 16
    unpackers, packers = [], []
    gate_lanes = jnp.zeros((slots, 128), jnp.float32)
    for p in range(passes):
        pieces = []
        for g in range(planes):
            gate = jnp.sum(jnp.where(lanes == plane + p * planes, meta[g], 0.0), axis=-1, keepdims=True)
            routed = jnp.where(gate != 0.0, 1.0, 0.0)
            earlier = jnp.sum(
                jnp.where(
                    lax.broadcasted_iota(jnp.int32, (8, 8), 0) < lax.broadcasted_iota(jnp.int32, (8, 8), 1), routed, 0.0
                ),
                axis=0, keepdims=True,
            )
            place = jnp.sum(jnp.where(diagonal, earlier, 0.0), axis=-1, keepdims=True).astype(jnp.int32)
            for h in range(2):
                pieces.append(jnp.where(lanes == place + (h * slots + g * cap), gate, 0.0))
        if count < 128:
            pieces.append(jnp.zeros((128 - count, 128), jnp.float32))
        spread = jnp.concatenate(pieces, axis=0)
        turned = spread.T
        unpackers.append(jnp.where(spread[:count, : 2 * slots] != 0.0, 1.0, 0.0).astype(jnp.bfloat16))
        packers.append(jnp.where(turned[: 2 * slots, :count] != 0.0, 1.0, 0.0).astype(jnp.bfloat16))
        slot_gate = jnp.sum(turned[:slots], axis=-1, keepdims=True)
        gate_lanes = gate_lanes + jnp.where(lax.broadcasted_iota(jnp.int32, (slots, 128), 1) == p, slot_gate, 0.0)
    slot_gates[chip] = gate_lanes
    slot = planes - 1
    for k in (3, 1, 2):
        src = slot_gates.at[chip]
        send(src, src, meta_send.at[slot + k - 1], meta_recv.at[slot + k - 1], mates[k])

    def meta_finish():
        for k in (1, 2, 3):
            src = slot_gates.at[mate[k]]
            remote(src, src, meta_send.at[slot + k - 1], meta_recv.at[slot + k - 1], mates[k]).wait_recv()

    for p in range(passes):
        if p > 0:
            gather_z(p)
        top_sum = bottom_sum = None
        for step in range(CHUNKS + 1):
            if step < CHUNKS:
                c = step
                for d in range(1, planes):
                    src = column.at[p, c, plane_at(-d)]
                    remote(src, src, zag_send.at[p, c, d - 1], zag_recv.at[p, c, d - 1], peers[d - 1]).wait_recv()
                if c + WINDOW < CHUNKS:
                    start_z(p, c + WINDOW)
                rows[p, c, chip] = jnp.dot(
                    packers[p], column[p, c].reshape(count, wide), preferred_element_type=jnp.float32
                ).astype(jnp.bfloat16)
                for k in (3, 1, 2):
                    src = rows.at[p, c, chip]
                    send(src, src, pag_send.at[p, c, k - 1], pag_recv.at[p, c, k - 1], mates[k])
            if step >= 1:
                c = step - 1
                for k in (1, 2, 3):
                    src = rows.at[p, c, mate[k]]
                    remote(src, src, pag_send.at[p, c, k - 1], pag_recv.at[p, c, k - 1], mates[k]).wait_recv()
                if p == 0 and c == 0:
                    locals_[0].wait()
                    up_copy.wait_recv()
                block = rows[p, c].reshape(CHIPS * 2 * slots, wide)
                top = jnp.dot(block, up[c * wide : (c + 1) * wide, :], preferred_element_type=jnp.float32)
                bottom = jnp.dot(
                    block, up[half + c * wide : half + (c + 1) * wide, :], preferred_element_type=jnp.float32
                )
                top_sum = top if c == 0 else top_sum + top
                bottom_sum = bottom if c == 0 else bottom_sum + bottom
        if p == 0:
            meta_finish()
            locals_[1].wait()
            down_copy.wait_recv()
        upward = (
            top_sum.reshape(CHIPS, 2, slots, 2 * HID_DEV)[:, 0]
            + bottom_sum.reshape(CHIPS, 2, slots, 2 * HID_DEV)[:, 1]
        ).reshape(CHIPS * slots, 2 * HID_DEV)
        gate = slot_gates[...].reshape(CHIPS * slots, 128)[:, p : p + 1]
        active = (upward / (1.0 + jnp.exp(-upward)) * gate).astype(jnp.bfloat16)

        def start_down(c):
            lo, hi = c * wide, (c + 1) * wide
            top = jnp.dot(active, down[:, lo:hi], preferred_element_type=jnp.float32)
            bottom = jnp.dot(active, down[:, half + lo : half + hi], preferred_element_type=jnp.float32)
            both = jnp.concatenate(
                [top.reshape(CHIPS, slots, wide), bottom.reshape(CHIPS, slots, wide)], axis=1
            )
            part[p, c] = both.astype(jnp.bfloat16)
            for k in (3, 1, 2):
                send(
                    part.at[p, c, mate[k]], first.at[p, c, k - 1],
                    one_send.at[p, c, k - 1], one_recv.at[p, c, k - 1], mates[k],
                )

        for c in range(WINDOW):
            start_down(c)
        for c in range(CHUNKS):
            total = part[p, c, chip].astype(jnp.float32)
            for k in (1, 2, 3):
                src = first.at[p, c, k - 1]
                remote(src, src, one_send.at[p, c, k - 1], one_recv.at[p, c, k - 1], mates[k]).wait_recv()
                total = total + first[p, c, k - 1].astype(jnp.float32)
            if c + WINDOW < CHUNKS:
                start_down(c + WINDOW)
            unpacked = jnp.dot(unpackers[p], total.astype(jnp.bfloat16), preferred_element_type=jnp.float32)
            plane_sum[p, c] = unpacked.astype(jnp.bfloat16).reshape(planes, 16, wide)
            for d in range(1, planes):
                send(
                    plane_sum.at[p, c, plane_at(d)], plane_in.at[p, c, d - 1],
                    zrs_send.at[p, c, d - 1], zrs_recv.at[p, c, d - 1], peers[d - 1],
                )
        for c in range(CHUNKS):
            lo, hi = c * wide, (c + 1) * wide
            total = plane_sum[p, c, plane].astype(jnp.float32)
            for d in range(1, planes):
                src = plane_in.at[p, c, d - 1]
                remote(src, src, zrs_send.at[p, c, d - 1], zrs_recv.at[p, c, d - 1], peers[d - 1]).wait_recv()
                total = total + plane_in[p, c, d - 1].astype(jnp.float32)
            for h in range(2):
                value = (cur[h, :, lo:hi] + total[h * 8 : h * 8 + 8]).astype(jnp.bfloat16).astype(jnp.float32)
                cur[h, :, lo:hi] = value
        if sections > 1:
            shift_out[p] = jnp.concatenate([cur[0], cur[1]], axis=0).astype(jnp.bfloat16)
            send(shift_out.at[p], shift_in.at[p], sh_send.at[p], sh_recv.at[p], after)
            remote(shift_out.at[p], shift_in.at[p], sh_send.at[p], sh_recv.at[p], after).wait_recv()
            for h in range(2):
                cur[h] = shift_in[p].astype(jnp.float32)[h * 8 : h * 8 + 8]
    for h in range(2):
        out[:, h * half : (h + 1) * half] = cur[h].astype(jnp.bfloat16)
    up_copy.wait_send()
    down_copy.wait_send()
    for copy in pending:
        copy.wait_send()


def body(hidden, norm_gain, w_up, w_down, expert_ids, route_gates):
    width = hidden.shape[-1]
    half = width // 2
    wide = half // CHUNKS
    planes = lax.axis_size("expert") // (2 * CHIPS)
    sections = lax.axis_size("section")
    passes = expert_ids.shape[1]
    bf = jnp.bfloat16
    dma = pltpu.SemaphoreType.DMA
    away = planes - 1
    shift = passes if sections > 1 else 1
    routes = hidden.shape[1] * expert_ids.shape[-1]
    cap = min(hidden.shape[1], (routes + planes - 1) // planes + 2)
    slots = planes * cap
    vmem = pl.BlockSpec(memory_space=pltpu.VMEM)
    hbm = pl.BlockSpec(memory_space=pl.ANY)
    result = pl.pallas_call(
        functools.partial(kernel, planes, sections, passes, cap),
        out_shape=jax.ShapeDtypeStruct((8, width), bf),
        in_specs=[vmem] * 4 + [hbm] * 2,
        out_specs=vmem,
        scratch_shapes=[
            pltpu.VMEM((width, 2 * HID_DEV), bf),
            pltpu.VMEM((2 * HID_DEV, width), bf),
            pltpu.VMEM((passes, CHUNKS, planes, 16, wide), bf),
            pltpu.VMEM((passes, CHUNKS, CHIPS, 2 * slots, wide), bf),
            pltpu.VMEM((planes, 8, 128), jnp.float32),
            pltpu.VMEM((CHIPS, slots, 128), jnp.float32),
            pltpu.VMEM((passes, CHUNKS, CHIPS, 2 * slots, wide), bf),
            pltpu.VMEM((passes, CHUNKS, 3, 2 * slots, wide), bf),
            pltpu.VMEM((passes, CHUNKS, planes, 16, wide), bf),
            pltpu.VMEM((passes, CHUNKS, away, 16, wide), bf),
            pltpu.VMEM((2, 8, half), jnp.float32),
            pltpu.VMEM((shift, 16, half), bf),
            pltpu.VMEM((shift, 16, half), bf),
            dma((2,)), dma((2,)), dma((2,)),
            dma((away + 3,)), dma((away + 3,)),
            dma((passes, CHUNKS, away)), dma((passes, CHUNKS, away)),
            dma((passes, CHUNKS, 3)), dma((passes, CHUNKS, 3)),
            dma((passes, CHUNKS, 3)), dma((passes, CHUNKS, 3)),
            dma((passes, CHUNKS, away)), dma((passes, CHUNKS, away)),
            dma((shift,)), dma((shift,)),
        ],
        compiler_params=pltpu.CompilerParams(
            collective_id=0, has_side_effects=True, vmem_limit_bytes=56 * 1024 * 1024
        ),
    )(
        hidden[0], norm_gain, expert_ids[0].swapaxes(1, 2), route_gates[0].swapaxes(1, 2), w_up[0], w_down[0]
    )
    return result[None]


def solution(mesh):
    placed = (
        P("section", "expert", None),
        P("section", None),
        P("section", None, "expert"),
        P("section", "expert", None),
        P("section", None, "expert", None),
        P("section", None, "expert", None),
    )
    return jax.shard_map(
        body, mesh=mesh, in_specs=placed, out_specs=P("section", "expert", None), check_vma=False
    )
```
